32 devices in a mesh: row: 8 (over z, x), col: 4 (over y, core).
Axes of the slice: x: 2, y: 2, z: 4, core: 2. Of those that a mesh axis runs over, the one named last changes fastest.
Arguments:
- signal: float32 [4096, 4096], P('row', 'col'), may hold values from -6 to 6
- apod: float32 [4096], P('row'), may hold values from 0.3 to 1
- coef: float32 [4, 4096], P(None, 'col'), may hold values from -0.5 to 1
- block_offset: int32 [128], P('col'), may hold values from -16 to 9
- fine_start: int32 [4096], P('col'), may hold values from 0 to 3
Outputs:
- calibrated: float32 [2, 4096, 4096], P(None, 'row', 'col')
The draws below stay inside these ranges and needn't reach their ends.
All inputs are finite; a program needn't handle non-finite values.
Results may differ from the reference program's by a relative error of at most 0.000084.
Values sent between devices are 32-bit elements; how exact they have to be, the bound alone decides.
No kernel may reach another device: no remote copies, remote signals or barrier semaphores. Data moves between devices by JAX's collectives and lax.ppermute only.
A program may use at most 128 MiB of HBM per device.

```python
import math
import jax
import jax.numpy as jnp

TLOC = 512
TAPS = 4
HALO = 16
CB = 32
T1 = 4096
COLS = 4096
NBLK = 128
N_ROW = 8


def with_ends(values, stream_key, least, largest):
    extent = values.shape
    index_at = [jax.random.randint(jax.random.fold_in(stream_key, axis), (), 0, extent[axis]) for axis in range(len(extent))]
    values = values.at[tuple(index_at)].set(least)
    longest = extent.index(max(extent))
    index_at[longest] = (index_at[longest] + 1) % extent[longest]
    return values.at[tuple(index_at)].set(largest)


def block_levels(own_key, extent, split, smallest, high):
    def one(dim, shards_of):
        heights = jax.random.uniform(jax.random.fold_in(jax.random.fold_in(own_key, 6), dim), (shards_of,), jnp.float32, smallest / len(split), high / len(split))
        return jnp.repeat(jnp.exp(heights), extent[dim] // shards_of).reshape((-1,) + (1,) * (len(extent) - dim - 1))

    loudness = one(*split[0])
    for cut in split[1:]:
        loudness = loudness * one(*cut)
    return loudness


def gaussian(own_key, dims, scale, limit, split=(), kind=jnp.bfloat16):
    entries = jax.random.normal(own_key, dims, jnp.float32) * scale
    if len(split) > 0:
        entries = block_levels(own_key, dims, split, -0.22, 0.18) * entries
    return jnp.clip(entries, min=-limit, max=limit).astype(kind)


def setup_inputs(seed: int = 0) -> dict:
    splits = jax.random.split(jax.random.key(seed), 6)
    signal = gaussian(splits[0], (T1, COLS), 1.0, 6.0, ((0, 8), (1, 4)), jnp.float32)
    apod = jnp.clip(0.3 + 0.7 * jax.random.uniform(splits[1], (T1,), jnp.float32) ** block_levels(splits[1], (T1,), ((0, 8),), -0.2, 0.2), 0.3, 1.0)
    coef = jnp.clip(-0.5 + 1.5 * jax.random.uniform(splits[2], (TAPS, COLS), jnp.float32) ** block_levels(splits[2], (TAPS, COLS), ((1, 4),), -0.2, 0.2), -0.5, 1.0)
    block_offset = with_ends(jax.random.randint(splits[3], (NBLK,), 0 - HALO, HALO - 2 * TAPS + 2), jax.random.fold_in(splits[3], 1), 0 - HALO, (HALO - 2 * TAPS + 2) - 1).astype(jnp.int32)
    fine_start = with_ends(jax.random.randint(splits[4], (COLS,), 0, TAPS), jax.random.fold_in(splits[4], 1), 0, TAPS - 1).astype(jnp.int32)
    return {"signal": signal, "apod": apod, "coef": coef, "block_offset": block_offset, "fine_start": fine_start}


def digits_reversed(values, levels):
    result = jnp.zeros_like(values)
    for digit in range(levels):
        result = result + ((values >> digit & 1) << levels - 1 - digit)
    return result

def stencil(field, coef, first):
    padded = jnp.pad(field, ((0, 0), (HALO, HALO)))
    total = jnp.zeros_like(field)
    for tap in range(TAPS):
        total = total + coef[tap][None, :] * jnp.take(padded, first + tap, axis=1)
    return total

def reference(signal, apod, coef, block_offset, fine_start):
    apodized = signal * apod[:, None]
    spectrum = jnp.fft.fft(apodized, axis=0) / math.sqrt(T1)
    levels = N_ROW.bit_length() - 1
    rowids = jnp.arange(T1, dtype=jnp.int32)
    freq = digits_reversed(rowids // TLOC, levels) + N_ROW * (rowids % TLOC)
    spectrum = jnp.take(spectrum, freq.astype(jnp.int32), axis=0)
    colids = jnp.arange(COLS, dtype=jnp.int32)
    first = colids + jnp.repeat(block_offset, CB) + fine_start + HALO
    real_part = stencil(jnp.real(spectrum).astype(signal.dtype), coef, first.astype(jnp.int32))
    imag_part = stencil(jnp.imag(spectrum).astype(signal.dtype), coef, first.astype(jnp.int32))
    return jnp.stack([real_part, imag_part])
```

```python
import functools
import math

import jax
import jax.numpy as jnp
import numpy as np
from jax import lax
from jax.experimental import pallas as pl
from jax.experimental.pallas import tpu as pltpu
from jax.sharding import PartitionSpec as P

TAPS = 4
LANES = 128
VMEM = 40 * 1024 * 1024


def split_bf16(value):
    high = value.astype(jnp.bfloat16)
    low = (value - high.astype(jnp.float32)).astype(jnp.bfloat16)
    return high, low


def dot3(a, b):
    dot = functools.partial(jnp.dot, preferred_element_type=jnp.float32)
    return dot(a[0], b[0]) + (dot(a[0], b[1]) + dot(a[1], b[0]))


def stencil_kernel(left, mid, right, apod, coef, offset, out):
    shape = (3 * LANES, LANES)
    tap_at = (
        lax.broadcasted_iota(jnp.int32, shape, 0)
        - lax.broadcasted_iota(jnp.int32, shape, 1)
        - LANES
        - offset[...]
    )
    band = jnp.zeros(shape, jnp.float32)
    for tap in range(TAPS):
        band = jnp.where(tap_at == tap, coef[tap : tap + 1, :], band)
    field = jnp.concatenate([left[...], mid[...], right[...]], axis=1)
    out[...] = apod[...] * dot3(split_bf16(field), split_bf16(band))


def stencil(left, mid, right, apod, coef, offset, block, count):
    rows = mid[0].shape[0]

    def columns(height, start):
        return pl.BlockSpec((height, LANES), lambda i: (0, start + i))

    return pl.pallas_call(
        stencil_kernel,
        grid=(count,),
        in_specs=[
            columns(rows, left[1]),
            columns(rows, mid[1]),
            columns(rows, right[1]),
            pl.BlockSpec((rows, 1), lambda i: (0, 0)),
            columns(TAPS, block),
            columns(1, block),
        ],
        out_specs=columns(rows, 0),
        out_shape=jax.ShapeDtypeStruct((rows, count * LANES), jnp.float32),
        compiler_params=pltpu.CompilerParams(vmem_limit_bytes=VMEM),
        cost_estimate=pl.CostEstimate(
            flops=6 * rows * 3 * LANES * LANES * count,
            bytes_accessed=16 * rows * LANES * count,
            transcendentals=0,
        ),
        name="stencil",
    )(left[0], mid[0], right[0], apod, coef, offset)


def inner_kernel(has_im, aliased, *refs):
    factors, cos_high, cos_low, sin_high, sin_low, *blocks = refs
    out = blocks.pop()
    if aliased:
        blocks.pop()
    a_re, a_im, b_re, b_im = (factors[:, i : i + 1] for i in range(4))
    if has_im:
        own_re, own_im, far_re, far_im = (ref[...] for ref in blocks)
        y_re = a_re * own_re - a_im * own_im + (b_re * far_re - b_im * far_im)
        y_im = a_re * own_im + a_im * own_re + (b_re * far_im + b_im * far_re)
    else:
        own_re, far_re = (ref[...] for ref in blocks)
        y_re = a_re * own_re + b_re * far_re
        y_im = a_im * own_re + b_im * far_re
    width = y_re.shape[1]
    both = split_bf16(jnp.concatenate([y_re, y_im], axis=1))
    cos_part = dot3((cos_high[...], cos_low[...]), both)
    sin_part = dot3((sin_high[...], sin_low[...]), both)
    out[0] = cos_part[:, :width] + sin_part[:, width:]
    out[1] = cos_part[:, width:] - sin_part[:, :width]


def inner(blocks, factors, tables, result, start, full_width):
    rows, width = blocks[0].shape
    aliased = result is not None
    whole = pl.BlockSpec((rows, rows), lambda i: (0, 0))
    step = width // LANES
    first = start // LANES
    inputs = [factors, *tables, *blocks] + ([result] if aliased else [])
    specs = (
        [pl.BlockSpec((rows, 4), lambda i: (0, 0))]
        + [whole] * 4
        + [pl.BlockSpec((rows, LANES), lambda i: (0, i))] * len(blocks)
        + ([pl.BlockSpec(memory_space=pl.ANY)] if aliased else [])
    )
    return pl.pallas_call(
        functools.partial(inner_kernel, len(blocks) == 4, aliased),
        grid=(step,),
        in_specs=specs,
        out_specs=pl.BlockSpec((2, rows, LANES), lambda i: (0, 0, first + i)),
        out_shape=jax.ShapeDtypeStruct((2, rows, full_width), jnp.float32),
        input_output_aliases={len(inputs) - 1: 0} if aliased else {},
        compiler_params=pltpu.CompilerParams(vmem_limit_bytes=VMEM),
        cost_estimate=pl.CostEstimate(
            flops=24 * rows * rows * width,
            bytes_accessed=4 * rows * width * 6 + 8 * rows * rows,
            transcendentals=0,
        ),
        name="inner",
    )(*inputs)


def reversed_bits(value, levels):
    return sum((value >> i & 1) << levels - 1 - i for i in range(levels))


def butterfly_plan(devices):
    stages = []
    phase = np.ones(devices, np.complex128)
    is_real = [True] * devices
    half = devices // 2
    while half:
        own, far = np.zeros(devices, np.complex128), np.zeros(devices, np.complex128)
        next_phase, next_real = phase.copy(), list(is_real)
        for a in range(devices):
            b = a ^ half
            upper = bool(a & half)
            turn = np.exp(-2j * np.pi * (a % half) / (2 * half)) if upper else 1.0
            keep = is_real[a] and phase[a] == 1 and phase[b] == 1
            if keep:
                own[a], far[a] = (-1 if upper else 1), 1
                next_phase[a] = turn
            else:
                own[a] = phase[a] * (-turn if upper else 1)
                far[a] = phase[b] * turn
                next_phase[a], next_real[a] = 1, False
        stages.append((half, own, far, [a for a in range(devices) if not is_real[a]], next_phase))
        phase, is_real = next_phase, next_real
        half //= 2
    return stages


def inner_tables(count, total):
    index = np.arange(count)
    angle = 2 * np.pi / count * (index[:, None] * index[None, :] % count)
    tables = []
    for part in (np.cos(angle), np.sin(angle)):
        part = part / math.sqrt(total)
        high = part.astype(jnp.bfloat16)
        tables += [high, (part - high.astype(np.float64)).astype(jnp.bfloat16)]
    return [jnp.asarray(t) for t in tables]


def parts(values):
    return np.stack([values.real, values.imag], -1).astype(np.float32)


def on_device(signal, apod, coef, block_offset, fine_start):
    rows, width = signal.shape
    devices, me = lax.axis_size("row"), lax.axis_index("row")
    levels = devices.bit_length() - 1
    total = rows * devices
    count = width // LANES
    spread = jnp.broadcast_to(
        block_offset[:, None], (block_offset.shape[0], width // block_offset.shape[0])
    ).reshape(width)
    offset = (spread + fine_start)[None, :]
    apod = apod[:, None]

    neighbours = lax.axis_size("col")
    up = [(i, i + 1) for i in range(neighbours - 1)]
    down = [(j, i) for i, j in up]
    before = lax.ppermute(signal[:, width - LANES :], "col", up)
    after = lax.ppermute(signal[:, :LANES], "col", down)

    stages = butterfly_plan(devices)
    tables = inner_tables(rows, total)
    outer = np.array([reversed_bits(a, levels) for a in range(devices)])
    twiddle = np.exp(-2j * np.pi / total * (outer[:, None] * np.arange(rows)[None, :] % total))
    _, own, far, _, phase = stages[-1]
    factors = np.concatenate(
        [parts((f * phase)[:, None] * twiddle) for f in (own, far)], axis=-1
    )
    factors = jnp.asarray(factors)[me]
    scalars = [
        jnp.asarray(np.concatenate([parts(s[1]), parts(s[2])], -1))[me] for s in stages[:-1]
    ]

    middle = list(range(1, count - 1))
    size = max(1, (len(middle) + 2) // 3)
    chunks = [(b, min(size, count - 1 - b)) for b in middle[::size]]
    fields = []
    for block, number in chunks:
        field = stencil(
            (signal, block - 1), (signal, block), (signal, block + 1), apod, coef, offset, block, number
        )
        fields.append((block, field))
    for block in (0, count - 1):
        left = (before, 0) if block == 0 else (signal, block - 1)
        right = (after, 0) if block == count - 1 else (signal, block + 1)
        field = stencil(left, (signal, block), right, apod, coef, offset, block, 1)
        fields.append((block, field))

    result = None
    for block, field in fields:
        real, imag = field, None
        for level, (half, own, far, complex_at, _) in enumerate(stages):
            everyone = [(a, a ^ half) for a in range(devices)]
            far_real = lax.ppermute(real, "row", everyone)
            far_imag = None
            if complex_at:
                far_imag = lax.ppermute(imag, "row", [(a, a ^ half) for a in complex_at])
            if level == levels - 1:
                break
            a_re, a_im, b_re, b_im = (scalars[level][i] for i in range(4))
            if far_imag is not None:
                real, imag = (
                    a_re * real - a_im * imag + (b_re * far_real - b_im * far_imag),
                    a_re * imag + a_im * real + (b_re * far_imag + b_im * far_real),
                )
            elif np.any(own.imag) or np.any(far.imag):
                real, imag = (a_re * real + b_re * far_real, a_im * real + b_im * far_real)
            else:
                real = a_re * real + b_re * far_real
        blocks = [real, far_real] if far_imag is None else [real, imag, far_real, far_imag]
        result = inner(blocks, factors, tables, result, block * LANES, width)
    return result


def solution(mesh):
    placed = (P("row", "col"), P("row"), P(None, "col"), P("col"), P("col"))
    return jax.shard_map(
        on_device, mesh=mesh, in_specs=placed, out_specs=P(None, "row", "col"), check_vma=False
    )
```

```python
import functools
import math

import jax
import jax.numpy as jnp
import numpy as np
from jax import lax
from jax.experimental import pallas as pl
from jax.experimental.pallas import tpu as pltpu
from jax.sharding import PartitionSpec as P

TAPS = 4
LANES = 128
AHEAD = 2
VMEM = 40 * 1024 * 1024
QUICK = pl.CostEstimate(flops=0, bytes_accessed=0, transcendentals=0)


def split_bf16(value):
    high = value.astype(jnp.bfloat16)
    low = (value - high.astype(jnp.float32)).astype(jnp.bfloat16)
    return high, low


def dot3(a, b):
    dot = functools.partial(jnp.dot, preferred_element_type=jnp.float32)
    return dot(a[0], b[0]) + (dot(a[0], b[1]) + dot(a[1], b[0]))


def stencil_kernel(block, per_block, offsets, left, mid, right, apod, coef, fine, *rest):
    out = rest[-1]
    rows = mid.shape[0]
    lane = lax.broadcasted_iota(jnp.int32, (1, LANES), 1)
    start = fine[...]
    if per_block >= LANES:
        start = start + offsets[block * LANES // per_block]
    else:
        for part in range(LANES // per_block):
            value = offsets[block * (LANES // per_block) + part]
            start = start + jnp.where(lane // per_block == part, value, 0)
    shape = (3 * LANES, LANES)
    tap_at = (
        lax.broadcasted_iota(jnp.int32, shape, 0)
        - lax.broadcasted_iota(jnp.int32, shape, 1)
        - LANES
        - start
    )
    band = jnp.zeros(shape, jnp.float32)
    for tap in range(TAPS):
        band = jnp.where(tap_at == tap, coef[tap : tap + 1, :], band)
    field = jnp.concatenate([left[...], mid[...], right[...]], axis=1)
    window = jnp.broadcast_to(apod[...], (LANES, rows)).T
    out[...] = window * dot3(split_bf16(field), split_bf16(band))


def stencil(left, mid, right, apod, coef, fine, offsets, block, after):
    rows, width = mid[0].shape

    def columns(height, at):
        return pl.BlockSpec((height, LANES), lambda i: (0, at))

    return pl.pallas_call(
        functools.partial(stencil_kernel, block, width // offsets.shape[0]),
        grid=(1,),
        in_specs=[pl.BlockSpec(memory_space=pltpu.SMEM)]
        + [columns(rows, at) for _, at in (left, mid, right)]
        + [
            pl.BlockSpec((1, rows), lambda i: (0, 0)),
            columns(TAPS, block),
            columns(1, block),
        ]
        + [pl.BlockSpec(memory_space=pl.ANY)] * len(after),
        out_specs=columns(rows, 0),
        out_shape=jax.ShapeDtypeStruct((rows, LANES), jnp.float32),
        compiler_params=pltpu.CompilerParams(vmem_limit_bytes=VMEM),
        cost_estimate=QUICK,
        name="stencil",
    )(offsets, left[0], mid[0], right[0], apod, coef, fine, *after)


def combine_kernel(me, factors, own, far, *rest):
    out = rest[-1]
    a_re, a_im, b_re, b_im = (factors[me[0], i] for i in range(4))
    if own.shape[0] == 2:
        out[0] = a_re * own[0] - a_im * own[1] + (b_re * far[0] - b_im * far[1])
        out[1] = a_re * own[1] + a_im * own[0] + (b_re * far[1] + b_im * far[0])
    elif out.shape[0] == 2:
        out[0] = a_re * own[0] + b_re * far[0]
        out[1] = a_im * own[0] + b_im * far[0]
    else:
        out[0] = a_re * own[0] + b_re * far[0]


def combine(me, factors, own, far, number, after):
    whole = pl.BlockSpec(memory_space=pltpu.VMEM)
    small = pl.BlockSpec(memory_space=pltpu.SMEM)
    return pl.pallas_call(
        combine_kernel,
        in_specs=[small, small, whole, whole] + [pl.BlockSpec(memory_space=pl.ANY)] * len(after),
        out_specs=whole,
        out_shape=jax.ShapeDtypeStruct((number,) + own.shape[1:], jnp.float32),
        compiler_params=pltpu.CompilerParams(vmem_limit_bytes=VMEM),
        cost_estimate=QUICK,
        name="combine",
    )(me, factors, own, far, *after)


def inner_kernel(me, factors, cos_high, cos_low, sin_high, sin_low, own, far, *rest):
    out, token = rest[-2:]
    a_re, a_im, b_re, b_im = (factors[0, :, i : i + 1] for i in range(4))
    if own.shape[0] == 2:
        y_re = a_re * own[0] - a_im * own[1] + (b_re * far[0] - b_im * far[1])
        y_im = a_re * own[1] + a_im * own[0] + (b_re * far[1] + b_im * far[0])
    else:
        y_re = a_re * own[0] + b_re * far[0]
        y_im = a_im * own[0] + b_im * far[0]
    both = split_bf16(jnp.concatenate([y_re, y_im], axis=1))
    cos_part = dot3((cos_high[...], cos_low[...]), both)
    sin_part = dot3((sin_high[...], sin_low[...]), both)
    out[0] = cos_part[:, :LANES] + sin_part[:, LANES:]
    out[1] = cos_part[:, LANES:] - sin_part[:, :LANES]
    token[...] = jnp.zeros_like(token)


def inner(me, factors, tables, own, far, result, block, full_width, after):
    number, rows, _ = own.shape
    kept = [] if result is None else [result]
    inputs = [me, factors, *tables, own, far, *after, *kept]
    specs = (
        [pl.BlockSpec((1, rows, 4), lambda i, at: (at[0], 0, 0))]
        + [pl.BlockSpec((rows, rows), lambda i, at: (0, 0))] * 4
        + [pl.BlockSpec((number, rows, LANES), lambda i, at: (0, 0, 0))] * 2
        + [pl.BlockSpec(memory_space=pl.ANY)] * (len(after) + len(kept))
    )
    return pl.pallas_call(
        inner_kernel,
        grid_spec=pltpu.PrefetchScalarGridSpec(
            num_scalar_prefetch=1,
            grid=(1,),
            in_specs=specs,
            out_specs=[
                pl.BlockSpec((2, rows, LANES), lambda i, at: (0, 0, block)),
                pl.BlockSpec((8, LANES), lambda i, at: (0, 0)),
            ],
        ),
        out_shape=[
            jax.ShapeDtypeStruct((2, rows, full_width), jnp.float32),
            jax.ShapeDtypeStruct((8, LANES), jnp.float32),
        ],
        input_output_aliases={len(inputs) - 1: 0} if kept else {},
        compiler_params=pltpu.CompilerParams(vmem_limit_bytes=VMEM),
        cost_estimate=QUICK,
        name="inner",
    )(*inputs)


def reversed_bits(value, levels):
    return sum((value >> i & 1) << levels - 1 - i for i in range(levels))


def butterfly_plan(devices):
    stages = []
    phase = np.ones(devices, np.complex128)
    is_real = [True] * devices
    half = devices // 2
    while half:
        own, far = np.zeros(devices, np.complex128), np.zeros(devices, np.complex128)
        next_phase, next_real = phase.copy(), list(is_real)
        for a in range(devices):
            b = a ^ half
            upper = bool(a & half)
            turn = np.exp(-2j * np.pi * (a % half) / (2 * half)) if upper else 1.0
            keep = is_real[a] and phase[a] == 1 and phase[b] == 1
            if keep:
                own[a], far[a] = (-1 if upper else 1), 1
                next_phase[a] = turn
            else:
                own[a] = phase[a] * (-turn if upper else 1)
                far[a] = phase[b] * turn
                next_phase[a], next_real[a] = 1, False
        stages.append((half, own, far, [a for a in range(devices) if not is_real[a]], next_phase))
        phase, is_real = next_phase, next_real
        half //= 2
    return stages


def inner_tables(count, total):
    index = np.arange(count)
    angle = 2 * np.pi / count * (index[:, None] * index[None, :] % count)
    tables = []
    for part in (np.cos(angle), np.sin(angle)):
        part = part / math.sqrt(total)
        high = part.astype(jnp.bfloat16)
        tables += [high, (part - high.astype(np.float64)).astype(jnp.bfloat16)]
    return [jnp.asarray(t) for t in tables]


def parts(*values):
    return np.stack([p for v in values for p in (v.real, v.imag)], -1).astype(np.float32)


def on_device(signal, apod, coef, block_offset, fine_start):
    rows, width = signal.shape
    devices = lax.axis_size("row")
    me = lax.axis_index("row").astype(jnp.int32)[None]
    levels = devices.bit_length() - 1
    total = rows * devices
    count = width // LANES

    neighbours = lax.axis_size("col")
    up = [(i, i + 1) for i in range(neighbours - 1)]
    down = [(j, i) for i, j in up]
    before = lax.ppermute(signal[:, width - LANES :], "col", up)
    behind = lax.ppermute(signal[:, :LANES], "col", down)

    stages = butterfly_plan(devices)
    tables = inner_tables(rows, total)
    outer = np.array([reversed_bits(a, levels) for a in range(devices)])
    twiddle = np.exp(-2j * np.pi / total * (outer[:, None] * np.arange(rows)[None, :] % total))
    factors = [jnp.asarray(parts(own, far)) for _, own, far, _, _ in stages[:-1]]
    _, own, far, _, phase = stages[-1]
    factors.append(
        jnp.asarray(parts((own * phase)[:, None] * twiddle, (far * phase)[:, None] * twiddle))
    )
    numbers = [2 if stages[s + 1][3] else 1 for s in range(levels - 1)]

    order = list(range(1, count - 1)) + [0, count - 1]

    def field_of(chunk, after):
        block = order[chunk]
        left = (before, 0) if block == 0 else (signal, block - 1)
        right = (behind, 0) if block == count - 1 else (signal, block + 1)
        field = stencil(
            left,
            (signal, block),
            right,
            apod[None, :],
            coef,
            fine_start[None, :],
            block_offset,
            block,
            after,
        )
        return field[None]

    def send(value, level):
        half = stages[level][0]
        return lax.ppermute(value, "row", [(a, a ^ half) for a in range(devices)])

    held, coming = {}, {}
    for chunk in range(min(AHEAD, count)):
        held[chunk] = field_of(chunk, [])
        coming[chunk] = send(held[chunk], 0)
    result, last = None, []
    for step in range(count + levels - 1):
        for level in range(levels):
            chunk = step - level
            if not 0 <= chunk < count:
                continue
            own, far = held.pop(chunk), coming.pop(chunk)
            if level < levels - 1:
                held[chunk] = combine(me, factors[level], own, far, numbers[level], last)
                coming[chunk] = send(held[chunk], level + 1)
                last = [held[chunk]]
            else:
                result, token = inner(
                    me, factors[level], tables, own, far, result, order[chunk], width, last
                )
                last = [token]
            if level == 0 and chunk + AHEAD < count:
                new = chunk + AHEAD
                held[new] = field_of(new, last)
                coming[new] = send(held[new], 0)
                last = [held[new]]
    return result


def solution(mesh):
    placed = (P("row", "col"), P("row"), P(None, "col"), P("col"), P("col"))
    return jax.shard_map(
        on_device, mesh=mesh, in_specs=placed, out_specs=P(None, "row", "col"), check_vma=False
    )
```

```python
import functools
import math

import jax
import jax.numpy as jnp
import numpy as np
from jax import lax
from jax.experimental import pallas as pl
from jax.experimental.pallas import tpu as pltpu
from jax.sharding import PartitionSpec as P

TAPS = 4
LANES = 128
AHEAD = 2
STENCIL_LATE = True
ORDER_INNER = None
SIZES = (1, 1, 1, 1, 1, 1)
ORDER = {0: [(1, -2)], 1: [(None, -3)], "between": [(0, 3)]}
VMEM = 40 * 1024 * 1024
QUICK = pl.CostEstimate(flops=0, bytes_accessed=0, transcendentals=0)


def split_bf16(value):
    high = value.astype(jnp.bfloat16)
    low = (value - high.astype(jnp.float32)).astype(jnp.bfloat16)
    return high, low


def dot3(a, b):
    dot = functools.partial(jnp.dot, preferred_element_type=jnp.float32)
    return dot(a[0], b[0]) + (dot(a[0], b[1]) + dot(a[1], b[0]))


def stencil_kernel(first, per_block, offsets, left, mid, right, apod, coef, fine, *rest):
    out = rest[-1]
    rows = mid.shape[0]
    block = first + pl.program_id(0)
    lane = lax.broadcasted_iota(jnp.int32, (1, LANES), 1)
    start = fine[...]
    if per_block >= LANES:
        start = start + offsets[block * LANES // per_block]
    else:
        for part in range(LANES // per_block):
            value = offsets[block * (LANES // per_block) + part]
            start = start + jnp.where(lane // per_block == part, value, 0)
    shape = (3 * LANES, LANES)
    tap_at = (
        lax.broadcasted_iota(jnp.int32, shape, 0)
        - lax.broadcasted_iota(jnp.int32, shape, 1)
        - LANES
        - start
    )
    band = jnp.zeros(shape, jnp.float32)
    for tap in range(TAPS):
        band = jnp.where(tap_at == tap, coef[tap : tap + 1, :], band)
    field = jnp.concatenate([left[...], mid[...], right[...]], axis=1)
    window = jnp.broadcast_to(apod[...], (LANES, rows)).T
    out[0] = window * dot3(split_bf16(field), split_bf16(band))


def stencil(left, mid, right, apod, coef, fine, offsets, block, count, after):
    rows, width = mid[0].shape

    def columns(height, at):
        return pl.BlockSpec((height, LANES), lambda i: (0, at + i))

    return pl.pallas_call(
        functools.partial(stencil_kernel, block, width // offsets.shape[0]),
        grid=(count,),
        in_specs=[pl.BlockSpec(memory_space=pltpu.SMEM)]
        + [columns(rows, at) for _, at in (left, mid, right)]
        + [
            pl.BlockSpec((1, rows), lambda i: (0, 0)),
            columns(TAPS, block),
            columns(1, block),
        ]
        + [pl.BlockSpec(memory_space=pl.ANY)] * len(after),
        out_specs=pl.BlockSpec((1, rows, LANES), lambda i: (0, 0, i)),
        out_shape=jax.ShapeDtypeStruct((1, rows, count * LANES), jnp.float32),
        compiler_params=pltpu.CompilerParams(vmem_limit_bytes=VMEM),
        cost_estimate=QUICK,
        name="stencil",
    )(offsets, left[0], mid[0], right[0], apod, coef, fine, *after)


def combine_kernel(me, factors, own, far, *rest):
    out = rest[-1]
    a_re, a_im, b_re, b_im = (factors[me[0], i] for i in range(4))
    if own.shape[0] == 2:
        out[0] = a_re * own[0] - a_im * own[1] + (b_re * far[0, 0] - b_im * far[0, 1])
        out[1] = a_re * own[1] + a_im * own[0] + (b_re * far[0, 1] + b_im * far[0, 0])
    elif out.shape[0] == 2:
        out[0] = a_re * own[0] + b_re * far[0, 0]
        out[1] = a_im * own[0] + b_im * far[0, 0]
    else:
        out[0] = a_re * own[0] + b_re * far[0, 0]


def combine(me, factors, own, far, half, number, after):
    shape = (number,) + own.shape[1:]
    return pl.pallas_call(
        combine_kernel,
        grid_spec=pltpu.PrefetchScalarGridSpec(
            num_scalar_prefetch=1,
            grid=(1,),
            in_specs=[
                pl.BlockSpec(memory_space=pltpu.SMEM),
                pl.BlockSpec(own.shape, lambda i, at: (0, 0, 0)),
                pl.BlockSpec((1,) + own.shape, lambda i, at: (1 - at[0] // half % 2, 0, 0, 0)),
            ]
            + [pl.BlockSpec(memory_space=pl.ANY)] * len(after),
            out_specs=pl.BlockSpec(shape, lambda i, at: (0, 0, 0)),
        ),
        out_shape=jax.ShapeDtypeStruct(shape, jnp.float32),
        compiler_params=pltpu.CompilerParams(vmem_limit_bytes=VMEM),
        cost_estimate=QUICK,
        name="combine",
    )(me, factors, own, far, *after)


def inner_kernel(me, factors, cos_high, cos_low, sin_high, sin_low, own, far, *rest):
    out, token = rest[-2:]
    a_re, a_im, b_re, b_im = (factors[0, :, i : i + 1] for i in range(4))
    if own.shape[0] == 2:
        y_re = a_re * own[0] - a_im * own[1] + (b_re * far[0, 0] - b_im * far[0, 1])
        y_im = a_re * own[1] + a_im * own[0] + (b_re * far[0, 1] + b_im * far[0, 0])
    else:
        y_re = a_re * own[0] + b_re * far[0, 0]
        y_im = a_im * own[0] + b_im * far[0, 0]
    both = split_bf16(jnp.concatenate([y_re, y_im], axis=1))
    cos_part = dot3((cos_high[...], cos_low[...]), both)
    sin_part = dot3((sin_high[...], sin_low[...]), both)
    out[0] = cos_part[:, :LANES] + sin_part[:, LANES:]
    out[1] = cos_part[:, LANES:] - sin_part[:, :LANES]
    token[...] = jnp.zeros_like(token)


def inner(me, factors, tables, own, far, result, block, full_width, after):
    number, rows, width = own.shape
    kept = [] if result is None else [result]
    inputs = [me, factors, *tables, own, far, *after, *kept]
    specs = (
        [pl.BlockSpec((1, rows, 4), lambda i, at: (at[0], 0, 0))]
        + [pl.BlockSpec((rows, rows), lambda i, at: (0, 0))] * 4
        + [
            pl.BlockSpec((number, rows, LANES), lambda i, at: (0, 0, i)),
            pl.BlockSpec((1, number, rows, LANES), lambda i, at: (1 - at[0] % 2, 0, 0, i)),
        ]
        + [pl.BlockSpec(memory_space=pl.ANY)] * (len(after) + len(kept))
    )
    return pl.pallas_call(
        inner_kernel,
        grid_spec=pltpu.PrefetchScalarGridSpec(
            num_scalar_prefetch=1,
            grid=(width // LANES,),
            in_specs=specs,
            out_specs=[
                pl.BlockSpec((2, rows, LANES), lambda i, at: (0, 0, block + i)),
                pl.BlockSpec((8, LANES), lambda i, at: (0, 0)),
            ],
        ),
        out_shape=[
            jax.ShapeDtypeStruct((2, rows, full_width), jnp.float32),
            jax.ShapeDtypeStruct((8, LANES), jnp.float32),
        ],
        input_output_aliases={len(inputs) - 1: 0} if kept else {},
        compiler_params=pltpu.CompilerParams(vmem_limit_bytes=VMEM),
        cost_estimate=QUICK,
        name="inner",
    )(*inputs)


def column_chunks(count):
    chunks, at = [], 1
    while at < count - 1:
        size = SIZES[min(len(chunks), len(SIZES) - 1)]
        chunks.append((at, min(size, count - 1 - at)))
        at += size
    return chunks + [(0, 1), (count - 1, 1)]


def reversed_bits(value, levels):
    return sum((value >> i & 1) << levels - 1 - i for i in range(levels))


def butterfly_plan(devices):
    stages = []
    phase = np.ones(devices, np.complex128)
    is_real = [True] * devices
    half = devices // 2
    while half:
        own, far = np.zeros(devices, np.complex128), np.zeros(devices, np.complex128)
        next_phase, next_real = phase.copy(), list(is_real)
        for a in range(devices):
            b = a ^ half
            upper = bool(a & half)
            turn = np.exp(-2j * np.pi * (a % half) / (2 * half)) if upper else 1.0
            keep = is_real[a] and phase[a] == 1 and phase[b] == 1
            if keep:
                own[a], far[a] = (-1 if upper else 1), 1
                next_phase[a] = turn
            else:
                own[a] = phase[a] * (-turn if upper else 1)
                far[a] = phase[b] * turn
                next_phase[a], next_real[a] = 1, False
        stages.append((half, own, far, [a for a in range(devices) if not is_real[a]], next_phase))
        phase, is_real = next_phase, next_real
        half //= 2
    return stages


def inner_tables(count, total):
    index = np.arange(count)
    angle = 2 * np.pi / count * (index[:, None] * index[None, :] % count)
    tables = []
    for part in (np.cos(angle), np.sin(angle)):
        part = part / math.sqrt(total)
        high = part.astype(jnp.bfloat16)
        tables += [high, (part - high.astype(np.float64)).astype(jnp.bfloat16)]
    return [jnp.asarray(t) for t in tables]


def parts(*values):
    return np.stack([p for v in values for p in (v.real, v.imag)], -1).astype(np.float32)


def on_device(signal, apod, coef, block_offset, fine_start):
    rows, width = signal.shape
    devices = lax.axis_size("row")
    me = lax.axis_index("row").astype(jnp.int32)[None]
    levels = devices.bit_length() - 1
    total = rows * devices
    count = width // LANES

    neighbours = lax.axis_size("col")
    up = [(i, i + 1) for i in range(neighbours - 1)]
    down = [(j, i) for i, j in up]
    before = lax.ppermute(signal[:, width - LANES :], "col", up)
    behind = lax.ppermute(signal[:, :LANES], "col", down)

    stages = butterfly_plan(devices)
    tables = inner_tables(rows, total)
    outer = np.array([reversed_bits(a, levels) for a in range(devices)])
    twiddle = np.exp(-2j * np.pi / total * (outer[:, None] * np.arange(rows)[None, :] % total))
    factors = [jnp.asarray(parts(own, far)) for _, own, far, _, _ in stages[:-1]]
    _, own, far, _, phase = stages[-1]
    factors.append(
        jnp.asarray(parts((own * phase)[:, None] * twiddle, (far * phase)[:, None] * twiddle))
    )
    numbers = [2 if stages[s + 1][3] else 1 for s in range(levels - 1)]

    chunks = column_chunks(count)

    def send(value, level):
        half = stages[level][0]
        pairs = [[a, a ^ half] for a in range(devices) if not a & half]
        return lax.all_gather(value, "row", axis_index_groups=pairs)

    out, far = {}, {}
    result = None

    def after(stage, chunk):
        rules = ORDER.get(stage, ORDER["between"] if 0 < stage < levels else [])
        wanted = [(levels if s is None else s, chunk + d) for s, d in rules]
        return [out[w] for w in wanted if w in out]

    for step in range(-AHEAD, len(chunks) + levels):
        for stage in [*range(1, levels), 0, levels] if STENCIL_LATE else range(levels + 1):
            chunk = step + AHEAD if stage == 0 else step - stage + 1
            if not 0 <= chunk < len(chunks):
                continue
            block, number = chunks[chunk]
            if stage == 0:
                left = (before, 0) if block == 0 else (signal, block - 1)
                right = (behind, 0) if block == count - 1 else (signal, block + 1)
                out[0, chunk] = stencil(
                    left,
                    (signal, block),
                    right,
                    apod[None, :],
                    coef,
                    fine_start[None, :],
                    block_offset,
                    block,
                    number,
                    after(0, chunk),
                )
            elif stage < levels:
                out[stage, chunk] = combine(
                    me,
                    factors[stage - 1],
                    out[stage - 1, chunk],
                    far[stage - 1, chunk],
                    stages[stage - 1][0],
                    numbers[stage - 1],
                    after(stage, chunk),
                )
            else:
                result, out[stage, chunk] = inner(
                    me,
                    factors[stage - 1],
                    tables,
                    out[stage - 1, chunk],
                    far[stage - 1, chunk],
                    result,
                    block,
                    width,
                    after(levels, chunk) if ORDER_INNER is None else [],
                )
            if stage < levels:
                far[stage, chunk] = send(out[stage, chunk], stage)
    return result


def solution(mesh):
    placed = (P("row", "col"), P("row"), P(None, "col"), P("col"), P("col"))
    return jax.shard_map(
        on_device, mesh=mesh, in_specs=placed, out_specs=P(None, "row", "col"), check_vma=False
    )
```

```python
import functools
import math

import jax
import jax.numpy as jnp
import numpy as np
from jax import lax
from jax.experimental import pallas as pl
from jax.experimental.pallas import tpu as pltpu
from jax.sharding import PartitionSpec as P

TAPS = 4
LANES = 128
SIZES = (1, 1, 1, 1, 1, 1)
ORDER = {
    "stencil": [],
    "gate": [("arrived", -1)],
    "first": [("inner", -3), ("middle", -2)],
    "middle": [("inner", -2)],
    "inner": [],
}
VMEM = 40 * 1024 * 1024
QUICK = pl.CostEstimate(flops=0, bytes_accessed=0, transcendentals=0)


def split_bf16(value):
    high = value.astype(jnp.bfloat16)
    low = (value - high.astype(jnp.float32)).astype(jnp.bfloat16)
    return high, low


def dot3(a, b):
    dot = functools.partial(jnp.dot, preferred_element_type=jnp.float32)
    return dot(a[0], b[0]) + (dot(a[0], b[1]) + dot(a[1], b[0]))


def stencil_kernel(first, per_block, offsets, left, mid, right, apod, coef, fine, *rest):
    out = rest[-1]
    rows = mid.shape[0]
    block = first + pl.program_id(0)
    lane = lax.broadcasted_iota(jnp.int32, (1, LANES), 1)
    start = fine[...]
    if per_block >= LANES:
        start = start + offsets[block * LANES // per_block]
    else:
        for part in range(LANES // per_block):
            value = offsets[block * (LANES // per_block) + part]
            start = start + jnp.where(lane // per_block == part, value, 0)
    shape = (3 * LANES, LANES)
    tap_at = (
        lax.broadcasted_iota(jnp.int32, shape, 0)
        - lax.broadcasted_iota(jnp.int32, shape, 1)
        - LANES
        - start
    )
    band = jnp.zeros(shape, jnp.float32)
    for tap in range(TAPS):
        band = jnp.where(tap_at == tap, coef[tap : tap + 1, :], band)
    field = jnp.concatenate([left[...], mid[...], right[...]], axis=1)
    window = jnp.broadcast_to(apod[...], (LANES, rows)).T
    out[0] = window * dot3(split_bf16(field), split_bf16(band))


def stencil(left, mid, right, apod, coef, fine, offsets, block, count, after):
    rows, width = mid[0].shape

    def columns(height, at):
        return pl.BlockSpec((height, LANES), lambda i: (0, at + i))

    return pl.pallas_call(
        functools.partial(stencil_kernel, block, width // offsets.shape[0]),
        grid=(count,),
        in_specs=[pl.BlockSpec(memory_space=pltpu.SMEM)]
        + [columns(rows, at) for _, at in (left, mid, right)]
        + [
            pl.BlockSpec((1, rows), lambda i: (0, 0)),
            columns(TAPS, block),
            columns(1, block),
        ]
        + [pl.BlockSpec(memory_space=pl.ANY)] * len(after),
        out_specs=pl.BlockSpec((1, rows, LANES), lambda i: (0, 0, i)),
        out_shape=jax.ShapeDtypeStruct((1, rows, count * LANES), jnp.float32),
        compiler_params=pltpu.CompilerParams(vmem_limit_bytes=VMEM),
        cost_estimate=QUICK,
        name="stencil",
    )(offsets, left[0], mid[0], right[0], apod, coef, fine, *after)


def gate_kernel(value, *rest):
    pass


def gate(value, after):
    anywhere = pl.BlockSpec(memory_space=pl.ANY)
    return pl.pallas_call(
        gate_kernel,
        in_specs=[anywhere] * (1 + len(after)),
        out_specs=anywhere,
        out_shape=jax.ShapeDtypeStruct(value.shape, value.dtype),
        input_output_aliases={0: 0},
        cost_estimate=QUICK,
        name="gate",
    )(value, *after)


def combine_kernel(me, factors, own, far, *rest):
    out = rest[-1]
    a_re, a_im, b_re, b_im = (factors[me[0], i] for i in range(4))
    if own.shape[0] == 2:
        out[0] = a_re * own[0] - a_im * own[1] + (b_re * far[0] - b_im * far[1])
        out[1] = a_re * own[1] + a_im * own[0] + (b_re * far[1] + b_im * far[0])
    elif out.shape[0] == 2:
        out[0] = a_re * own[0] + b_re * far[0]
        out[1] = a_im * own[0] + b_im * far[0]
    else:
        out[0] = a_re * own[0] + b_re * far[0]


def combine(me, factors, own, far, number, after):
    whole = pl.BlockSpec(memory_space=pltpu.VMEM)
    small = pl.BlockSpec(memory_space=pltpu.SMEM)
    return pl.pallas_call(
        combine_kernel,
        in_specs=[small, small, whole, whole] + [pl.BlockSpec(memory_space=pl.ANY)] * len(after),
        out_specs=whole,
        out_shape=jax.ShapeDtypeStruct((number,) + own.shape[1:], jnp.float32),
        compiler_params=pltpu.CompilerParams(vmem_limit_bytes=VMEM),
        cost_estimate=QUICK,
        name="combine",
    )(me, factors, own, far, *after)


def inner_kernel(me, factors, cos_high, cos_low, sin_high, sin_low, own, far, *rest):
    out, token = rest[-2:]
    a_re, a_im, b_re, b_im = (factors[0, :, i : i + 1] for i in range(4))
    if own.shape[0] == 2:
        y_re = a_re * own[0] - a_im * own[1] + (b_re * far[0] - b_im * far[1])
        y_im = a_re * own[1] + a_im * own[0] + (b_re * far[1] + b_im * far[0])
    else:
        y_re = a_re * own[0] + b_re * far[0]
        y_im = a_im * own[0] + b_im * far[0]
    both = split_bf16(jnp.concatenate([y_re, y_im], axis=1))
    cos_part = dot3((cos_high[...], cos_low[...]), both)
    sin_part = dot3((sin_high[...], sin_low[...]), both)
    out[0] = cos_part[:, :LANES] + sin_part[:, LANES:]
    out[1] = cos_part[:, LANES:] - sin_part[:, :LANES]
    token[...] = jnp.zeros_like(token)


def inner(me, factors, tables, own, far, result, block, full_width, after):
    number, rows, width = own.shape
    kept = [] if result is None else [result]
    inputs = [me, factors, *tables, own, far, *after, *kept]
    specs = (
        [pl.BlockSpec((1, rows, 4), lambda i, at: (at[0], 0, 0))]
        + [pl.BlockSpec((rows, rows), lambda i, at: (0, 0))] * 4
        + [pl.BlockSpec((number, rows, LANES), lambda i, at: (0, 0, i))] * 2
        + [pl.BlockSpec(memory_space=pl.ANY)] * (len(after) + len(kept))
    )
    return pl.pallas_call(
        inner_kernel,
        grid_spec=pltpu.PrefetchScalarGridSpec(
            num_scalar_prefetch=1,
            grid=(width // LANES,),
            in_specs=specs,
            out_specs=[
                pl.BlockSpec((2, rows, LANES), lambda i, at: (0, 0, block + i)),
                pl.BlockSpec((8, LANES), lambda i, at: (0, 0)),
            ],
        ),
        out_shape=[
            jax.ShapeDtypeStruct((2, rows, full_width), jnp.float32),
            jax.ShapeDtypeStruct((8, LANES), jnp.float32),
        ],
        input_output_aliases={len(inputs) - 1: 0} if kept else {},
        compiler_params=pltpu.CompilerParams(vmem_limit_bytes=VMEM),
        cost_estimate=QUICK,
        name="inner",
    )(*inputs)


def column_chunks(count):
    chunks, at = [], 1
    while at < count - 1:
        size = SIZES[min(len(chunks), len(SIZES) - 1)]
        chunks.append((at, min(size, count - 1 - at)))
        at += size
    return chunks + [(0, 1), (count - 1, 1)]


def reversed_bits(value, levels):
    return sum((value >> i & 1) << levels - 1 - i for i in range(levels))


def butterfly_plan(devices):
    stages = []
    phase = np.ones(devices, np.complex128)
    is_real = [True] * devices
    half = devices // 2
    while half:
        own, far = np.zeros(devices, np.complex128), np.zeros(devices, np.complex128)
        next_phase, next_real = phase.copy(), list(is_real)
        for a in range(devices):
            b = a ^ half
            upper = bool(a & half)
            turn = np.exp(-2j * np.pi * (a % half) / (2 * half)) if upper else 1.0
            keep = is_real[a] and phase[a] == 1 and phase[b] == 1
            if keep:
                own[a], far[a] = (-1 if upper else 1), 1
                next_phase[a] = turn
            else:
                own[a] = phase[a] * (-turn if upper else 1)
                far[a] = phase[b] * turn
                next_phase[a], next_real[a] = 1, False
        stages.append((half, own, far, [a for a in range(devices) if not is_real[a]], next_phase))
        phase, is_real = next_phase, next_real
        half //= 2
    return stages


def inner_tables(count, total):
    index = np.arange(count)
    angle = 2 * np.pi / count * (index[:, None] * index[None, :] % count)
    tables = []
    for part in (np.cos(angle), np.sin(angle)):
        part = part / math.sqrt(total)
        high = part.astype(jnp.bfloat16)
        tables += [high, (part - high.astype(np.float64)).astype(jnp.bfloat16)]
    return [jnp.asarray(t) for t in tables]


def parts(*values):
    return np.stack([p for v in values for p in (v.real, v.imag)], -1).astype(np.float32)


def on_device(signal, apod, coef, block_offset, fine_start):
    rows, width = signal.shape
    devices = lax.axis_size("row")
    me = lax.axis_index("row").astype(jnp.int32)[None]
    levels = devices.bit_length() - 1
    total = rows * devices
    count = width // LANES

    neighbours = lax.axis_size("col")
    up = [(i, i + 1) for i in range(neighbours - 1)]
    down = [(j, i) for i, j in up]
    before = lax.ppermute(signal[:, width - LANES :], "col", up)
    behind = lax.ppermute(signal[:, :LANES], "col", down)

    stages = butterfly_plan(devices)
    tables = inner_tables(rows, total)
    outer = np.array([reversed_bits(a, levels) for a in range(devices)])
    twiddle = np.exp(-2j * np.pi / total * (outer[:, None] * np.arange(rows)[None, :] % total))
    factors = [jnp.asarray(parts(own, far)) for _, own, far, _, _ in stages[:-1]]
    _, own, far, _, phase = stages[-1]
    factors.append(
        jnp.asarray(parts((own * phase)[:, None] * twiddle, (far * phase)[:, None] * twiddle))
    )
    numbers = [2 if stages[s + 1][3] else 1 for s in range(levels - 1)]

    chunks = column_chunks(count)

    def send(value, level):
        half = stages[level][0]
        return lax.ppermute(value, "row", [(a, a ^ half) for a in range(devices)])

    out, far, results = {}, {}, {}
    stage_of = {"stencil": 0, "first": 1, "middle": levels - 1, "inner": levels}

    def after(name, chunk):
        kept = []
        for what, shift in ORDER[name]:
            at = chunk + shift
            if 0 <= at < len(chunks):
                if what == "arrived":
                    make(0, at)
                    kept.append(far[0, at])
                else:
                    make(stage_of[what], at)
                    kept.append(out[stage_of[what], at])
        return kept

    def make(stage, chunk):
        if (stage, chunk) in out:
            return
        block, number = chunks[chunk]
        if stage == 0:
            left = (before, 0) if block == 0 else (signal, block - 1)
            right = (behind, 0) if block == count - 1 else (signal, block + 1)
            out[stage, chunk] = stencil(
                left,
                (signal, block),
                right,
                apod[None, :],
                coef,
                fine_start[None, :],
                block_offset,
                block,
                number,
                after("stencil", chunk),
            )
            waits = after("gate", chunk)
            if waits:
                out[stage, chunk] = gate(out[stage, chunk], waits)
        else:
            make(stage - 1, chunk)
            near = (out[stage - 1, chunk], far[stage - 1, chunk])
            if stage < levels:
                out[stage, chunk] = combine(
                    me,
                    factors[stage - 1],
                    *near,
                    numbers[stage - 1],
                    after("first" if stage == 1 else "middle", chunk),
                )
            else:
                if chunk:
                    make(stage, chunk - 1)
                results[chunk], out[stage, chunk] = inner(
                    me,
                    factors[stage - 1],
                    tables,
                    *near,
                    results.get(chunk - 1),
                    block,
                    width,
                    after("inner", chunk),
                )
        if stage < levels:
            far[stage, chunk] = send(out[stage, chunk], stage)

    make(levels, len(chunks) - 1)
    return results[len(chunks) - 1]


def solution(mesh):
    placed = (P("row", "col"), P("row"), P(None, "col"), P("col"), P("col"))
    return jax.shard_map(
        on_device, mesh=mesh, in_specs=placed, out_specs=P(None, "row", "col"), check_vma=False
    )
```

```python
import functools
import math

import jax
import jax.numpy as jnp
import numpy as np
from jax import lax
from jax.experimental import pallas as pl
from jax.experimental.pallas import tpu as pltpu
from jax.sharding import PartitionSpec as P

TAPS = 4
LANES = 128
SIZES = (1, 1, 1, 1, 1, 1)
ORDER = {
    "stencil": [],
    "gate": [("arrived", -1)],
    "first": [("inner", -3)],
    "middle": [("stencil", 2), ("inner", -2)],
    "inner": [],
}
MIB = 1024 * 1024
VMEM = 20 * MIB
GATE_VMEM = 1 * MIB
FIRST_VMEM = 56 * MIB
QUICK = pl.CostEstimate(flops=0, bytes_accessed=0, transcendentals=0)


def split_bf16(value):
    high = value.astype(jnp.bfloat16)
    low = (value - high.astype(jnp.float32)).astype(jnp.bfloat16)
    return high, low


def dot3(a, b):
    dot = functools.partial(jnp.dot, preferred_element_type=jnp.float32)
    return dot(a[0], b[0]) + (dot(a[0], b[1]) + dot(a[1], b[0]))


def stencil_kernel(first, per_block, offsets, left, mid, right, apod, coef, fine, *rest):
    out = rest[-1]
    rows = mid.shape[0]
    block = first + pl.program_id(0)
    lane = lax.broadcasted_iota(jnp.int32, (1, LANES), 1)
    start = fine[...]
    if per_block >= LANES:
        start = start + offsets[block * LANES // per_block]
    else:
        for part in range(LANES // per_block):
            value = offsets[block * (LANES // per_block) + part]
            start = start + jnp.where(lane // per_block == part, value, 0)
    shape = (3 * LANES, LANES)
    tap_at = (
        lax.broadcasted_iota(jnp.int32, shape, 0)
        - lax.broadcasted_iota(jnp.int32, shape, 1)
        - LANES
        - start
    )
    band = jnp.zeros(shape, jnp.float32)
    for tap in range(TAPS):
        band = jnp.where(tap_at == tap, coef[tap : tap + 1, :], band)
    field = jnp.concatenate([left[...], mid[...], right[...]], axis=1)
    window = jnp.broadcast_to(apod[...], (LANES, rows)).T
    out[0] = window * dot3(split_bf16(field), split_bf16(band))


def stencil(left, mid, right, apod, coef, fine, offsets, block, count, after, vmem=VMEM):
    rows, width = mid[0].shape

    def columns(height, at):
        return pl.BlockSpec((height, LANES), lambda i: (0, at + i))

    return pl.pallas_call(
        functools.partial(stencil_kernel, block, width // offsets.shape[0]),
        grid=(count,),
        in_specs=[pl.BlockSpec(memory_space=pltpu.SMEM)]
        + [columns(rows, at) for _, at in (left, mid, right)]
        + [
            pl.BlockSpec((1, rows), lambda i: (0, 0)),
            columns(TAPS, block),
            columns(1, block),
        ]
        + [pl.BlockSpec(memory_space=pl.ANY)] * len(after),
        out_specs=pl.BlockSpec((1, rows, LANES), lambda i: (0, 0, i)),
        out_shape=jax.ShapeDtypeStruct((1, rows, count * LANES), jnp.float32),
        compiler_params=pltpu.CompilerParams(vmem_limit_bytes=vmem),
        cost_estimate=QUICK,
        name="stencil",
    )(offsets, left[0], mid[0], right[0], apod, coef, fine, *after)


def gate_kernel(value, *rest):
    pass


def gate(value, after):
    anywhere = pl.BlockSpec(memory_space=pl.ANY)
    return pl.pallas_call(
        gate_kernel,
        in_specs=[anywhere] * (1 + len(after)),
        out_specs=anywhere,
        out_shape=jax.ShapeDtypeStruct(value.shape, value.dtype),
        input_output_aliases={0: 0},
        compiler_params=pltpu.CompilerParams(vmem_limit_bytes=GATE_VMEM),
        cost_estimate=QUICK,
        name="gate",
    )(value, *after)


def combine_kernel(me, factors, own, far, *rest):
    out = rest[-1]
    a_re, a_im, b_re, b_im = (factors[me[0], i] for i in range(4))
    if own.shape[0] == 2:
        out[0] = a_re * own[0] - a_im * own[1] + (b_re * far[0] - b_im * far[1])
        out[1] = a_re * own[1] + a_im * own[0] + (b_re * far[1] + b_im * far[0])
    elif out.shape[0] == 2:
        out[0] = a_re * own[0] + b_re * far[0]
        out[1] = a_im * own[0] + b_im * far[0]
    else:
        out[0] = a_re * own[0] + b_re * far[0]


def combine(me, factors, own, far, number, after):
    whole = pl.BlockSpec(memory_space=pltpu.VMEM)
    small = pl.BlockSpec(memory_space=pltpu.SMEM)
    return pl.pallas_call(
        combine_kernel,
        in_specs=[small, small, whole, whole] + [pl.BlockSpec(memory_space=pl.ANY)] * len(after),
        out_specs=whole,
        out_shape=jax.ShapeDtypeStruct((number,) + own.shape[1:], jnp.float32),
        compiler_params=pltpu.CompilerParams(vmem_limit_bytes=VMEM),
        cost_estimate=QUICK,
        name="combine",
    )(me, factors, own, far, *after)


def inner_kernel(me, factors, cos_high, cos_low, sin_high, sin_low, own, far, *rest):
    out, token = rest[-2:]
    a_re, a_im, b_re, b_im = (factors[0, :, i : i + 1] for i in range(4))
    if own.shape[0] == 2:
        y_re = a_re * own[0] - a_im * own[1] + (b_re * far[0] - b_im * far[1])
        y_im = a_re * own[1] + a_im * own[0] + (b_re * far[1] + b_im * far[0])
    else:
        y_re = a_re * own[0] + b_re * far[0]
        y_im = a_im * own[0] + b_im * far[0]
    both = split_bf16(jnp.concatenate([y_re, y_im], axis=1))
    cos_part = dot3((cos_high[...], cos_low[...]), both)
    sin_part = dot3((sin_high[...], sin_low[...]), both)
    out[0] = cos_part[:, :LANES] + sin_part[:, LANES:]
    out[1] = cos_part[:, LANES:] - sin_part[:, :LANES]
    token[...] = jnp.zeros_like(token)


def inner(me, factors, tables, own, far, result, block, full_width, after):
    number, rows, width = own.shape
    kept = [] if result is None else [result]
    inputs = [me, factors, *tables, own, far, *after, *kept]
    specs = (
        [pl.BlockSpec((1, rows, 4), lambda i, at: (at[0], 0, 0))]
        + [pl.BlockSpec((rows, rows), lambda i, at: (0, 0))] * 4
        + [pl.BlockSpec((number, rows, LANES), lambda i, at: (0, 0, i))] * 2
        + [pl.BlockSpec(memory_space=pl.ANY)] * (len(after) + len(kept))
    )
    return pl.pallas_call(
        inner_kernel,
        grid_spec=pltpu.PrefetchScalarGridSpec(
            num_scalar_prefetch=1,
            grid=(width // LANES,),
            in_specs=specs,
            out_specs=[
                pl.BlockSpec((2, rows, LANES), lambda i, at: (0, 0, block + i)),
                pl.BlockSpec((8, LANES), lambda i, at: (0, 0)),
            ],
        ),
        out_shape=[
            jax.ShapeDtypeStruct((2, rows, full_width), jnp.float32),
            jax.ShapeDtypeStruct((8, LANES), jnp.float32),
        ],
        input_output_aliases={len(inputs) - 1: 0} if kept else {},
        compiler_params=pltpu.CompilerParams(vmem_limit_bytes=VMEM),
        cost_estimate=QUICK,
        name="inner",
    )(*inputs)


def column_chunks(count):
    chunks, at = [], 1
    while at < count - 1:
        size = SIZES[min(len(chunks), len(SIZES) - 1)]
        chunks.append((at, min(size, count - 1 - at)))
        at += size
    return chunks + [(0, 1), (count - 1, 1)]


def reversed_bits(value, levels):
    return sum((value >> i & 1) << levels - 1 - i for i in range(levels))


def butterfly_plan(devices):
    stages = []
    phase = np.ones(devices, np.complex128)
    is_real = [True] * devices
    half = devices // 2
    while half:
        own, far = np.zeros(devices, np.complex128), np.zeros(devices, np.complex128)
        next_phase, next_real = phase.copy(), list(is_real)
        for a in range(devices):
            b = a ^ half
            upper = bool(a & half)
            turn = np.exp(-2j * np.pi * (a % half) / (2 * half)) if upper else 1.0
            keep = is_real[a] and phase[a] == 1 and phase[b] == 1
            if keep:
                own[a], far[a] = (-1 if upper else 1), 1
                next_phase[a] = turn
            else:
                own[a] = phase[a] * (-turn if upper else 1)
                far[a] = phase[b] * turn
                next_phase[a], next_real[a] = 1, False
        stages.append((half, own, far, [a for a in range(devices) if not is_real[a]], next_phase))
        phase, is_real = next_phase, next_real
        half //= 2
    return stages


def inner_tables(count, total):
    index = np.arange(count)
    angle = 2 * np.pi / count * (index[:, None] * index[None, :] % count)
    tables = []
    for part in (np.cos(angle), np.sin(angle)):
        part = part / math.sqrt(total)
        high = part.astype(jnp.bfloat16)
        tables += [high, (part - high.astype(np.float64)).astype(jnp.bfloat16)]
    return [jnp.asarray(t) for t in tables]


def parts(*values):
    return np.stack([p for v in values for p in (v.real, v.imag)], -1).astype(np.float32)


def on_device(signal, apod, coef, block_offset, fine_start):
    rows, width = signal.shape
    devices = lax.axis_size("row")
    me = lax.axis_index("row").astype(jnp.int32)[None]
    levels = devices.bit_length() - 1
    total = rows * devices
    count = width // LANES

    neighbours = lax.axis_size("col")
    up = [(i, i + 1) for i in range(neighbours - 1)]
    down = [(j, i) for i, j in up]
    before = lax.ppermute(signal[:, width - LANES :], "col", up)
    behind = lax.ppermute(signal[:, :LANES], "col", down)

    stages = butterfly_plan(devices)
    tables = inner_tables(rows, total)
    outer = np.array([reversed_bits(a, levels) for a in range(devices)])
    twiddle = np.exp(-2j * np.pi / total * (outer[:, None] * np.arange(rows)[None, :] % total))
    factors = [jnp.asarray(parts(own, far)) for _, own, far, _, _ in stages[:-1]]
    _, own, far, _, phase = stages[-1]
    factors.append(
        jnp.asarray(parts((own * phase)[:, None] * twiddle, (far * phase)[:, None] * twiddle))
    )
    numbers = [2 if stages[s + 1][3] else 1 for s in range(levels - 1)]

    chunks = column_chunks(count)

    def send(value, level):
        half = stages[level][0]
        return lax.ppermute(value, "row", [(a, a ^ half) for a in range(devices)])

    out, far, results = {}, {}, {}
    stage_of = {"stencil": 0, "first": 1, "middle": levels - 1, "inner": levels}

    def after(name, chunk):
        kept = []
        for what, shift in ORDER[name]:
            at = chunk + shift
            if 0 <= at < len(chunks):
                if what == "arrived":
                    make(0, at)
                    kept.append(far[0, at])
                else:
                    make(stage_of[what], at)
                    kept.append(out[stage_of[what], at])
        return kept

    def make(stage, chunk):
        if (stage, chunk) in out:
            return
        block, number = chunks[chunk]
        if stage == 0:
            left = (before, 0) if block == 0 else (signal, block - 1)
            right = (behind, 0) if block == count - 1 else (signal, block + 1)
            out[stage, chunk] = stencil(
                left,
                (signal, block),
                right,
                apod[None, :],
                coef,
                fine_start[None, :],
                block_offset,
                block,
                number,
                after("stencil", chunk),
                VMEM if chunk else FIRST_VMEM,
            )
            waits = after("gate", chunk)
            if waits:
                out[stage, chunk] = gate(out[stage, chunk], waits)
        else:
            make(stage - 1, chunk)
            near = (out[stage - 1, chunk], far[stage - 1, chunk])
            if stage < levels:
                out[stage, chunk] = combine(
                    me,
                    factors[stage - 1],
                    *near,
                    numbers[stage - 1],
                    after("first" if stage == 1 else "middle", chunk),
                )
            else:
                if chunk:
                    make(stage, chunk - 1)
                results[chunk], out[stage, chunk] = inner(
                    me,
                    factors[stage - 1],
                    tables,
                    *near,
                    results.get(chunk - 1),
                    block,
                    width,
                    after("inner", chunk),
                )
        if stage < levels:
            far[stage, chunk] = send(out[stage, chunk], stage)

    make(levels, len(chunks) - 1)
    return results[len(chunks) - 1]


def solution(mesh):
    placed = (P("row", "col"), P("row"), P(None, "col"), P("col"), P("col"))
    return jax.shard_map(
        on_device, mesh=mesh, in_specs=placed, out_specs=P(None, "row", "col"), check_vma=False
    )
```

```python
import functools
import math

import jax
import jax.numpy as jnp
import numpy as np
from jax import lax
from jax.experimental import pallas as pl
from jax.experimental.pallas import tpu as pltpu
from jax.sharding import PartitionSpec as P

TAPS = 4
LANES = 128
DIRECT = 2
SIZES = (1, 1, 1, 1, 1, 1)
ORDER = {
    "stencil": [],
    "gate": [("arrived", -1)],
    "first": [("inner", -3)],
    "middle": [("stencil", 2), ("inner", -2)],
    "inner": [],
}
MIB = 1024 * 1024
VMEM = 20 * MIB
GATE_VMEM = 1 * MIB
FIRST_VMEM = 56 * MIB
QUICK = pl.CostEstimate(flops=0, bytes_accessed=0, transcendentals=0)


def split_bf16(value):
    high = value.astype(jnp.bfloat16)
    low = (value - high.astype(jnp.float32)).astype(jnp.bfloat16)
    return high, low


def dot3(a, b):
    dot = functools.partial(jnp.dot, preferred_element_type=jnp.float32)
    return dot(a[0], b[0]) + (dot(a[0], b[1]) + dot(a[1], b[0]))


def stencil_kernel(first, per_block, offsets, left, mid, right, apod, coef, fine, *rest):
    out = rest[-1]
    rows = mid.shape[0]
    block = first + pl.program_id(0)
    lane = lax.broadcasted_iota(jnp.int32, (1, LANES), 1)
    start = fine[...]
    if per_block >= LANES:
        start = start + offsets[block * LANES // per_block]
    else:
        for part in range(LANES // per_block):
            value = offsets[block * (LANES // per_block) + part]
            start = start + jnp.where(lane // per_block == part, value, 0)
    shape = (3 * LANES, LANES)
    tap_at = (
        lax.broadcasted_iota(jnp.int32, shape, 0)
        - lax.broadcasted_iota(jnp.int32, shape, 1)
        - LANES
        - start
    )
    band = jnp.zeros(shape, jnp.float32)
    for tap in range(TAPS):
        band = jnp.where(tap_at == tap, coef[tap : tap + 1, :], band)
    field = jnp.concatenate([left[...], mid[...], right[...]], axis=1)
    window = jnp.broadcast_to(apod[...], (LANES, rows)).T
    out[0] = window * dot3(split_bf16(field), split_bf16(band))


def stencil(left, mid, right, apod, coef, fine, offsets, block, count, after, vmem=VMEM):
    rows, width = mid[0].shape

    def columns(height, at):
        return pl.BlockSpec((height, LANES), lambda i: (0, at + i))

    return pl.pallas_call(
        functools.partial(stencil_kernel, block, width // offsets.shape[0]),
        grid=(count,),
        in_specs=[pl.BlockSpec(memory_space=pltpu.SMEM)]
        + [columns(rows, at) for _, at in (left, mid, right)]
        + [
            pl.BlockSpec((1, rows), lambda i: (0, 0)),
            columns(TAPS, block),
            columns(1, block),
        ]
        + [pl.BlockSpec(memory_space=pl.ANY)] * len(after),
        out_specs=pl.BlockSpec((1, rows, LANES), lambda i: (0, 0, i)),
        out_shape=jax.ShapeDtypeStruct((1, rows, count * LANES), jnp.float32),
        compiler_params=pltpu.CompilerParams(vmem_limit_bytes=vmem),
        cost_estimate=QUICK,
        name="stencil",
    )(offsets, left[0], mid[0], right[0], apod, coef, fine, *after)


def gate_kernel(value, *rest):
    pass


def gate(value, after):
    anywhere = pl.BlockSpec(memory_space=pl.ANY)
    return pl.pallas_call(
        gate_kernel,
        in_specs=[anywhere] * (1 + len(after)),
        out_specs=anywhere,
        out_shape=jax.ShapeDtypeStruct(value.shape, value.dtype),
        input_output_aliases={0: 0},
        compiler_params=pltpu.CompilerParams(vmem_limit_bytes=GATE_VMEM),
        cost_estimate=QUICK,
        name="gate",
    )(value, *after)


def combine_kernel(me, factors, own, far, *rest):
    out = rest[-1]
    a_re, a_im, b_re, b_im = (factors[me[0], i] for i in range(4))
    if own.shape[0] == 2:
        out[0] = a_re * own[0] - a_im * own[1] + (b_re * far[0] - b_im * far[1])
        out[1] = a_re * own[1] + a_im * own[0] + (b_re * far[1] + b_im * far[0])
    elif out.shape[0] == 2:
        out[0] = a_re * own[0] + b_re * far[0]
        out[1] = a_im * own[0] + b_im * far[0]
    else:
        out[0] = a_re * own[0] + b_re * far[0]


def combine(me, factors, own, far, number, after):
    whole = pl.BlockSpec(memory_space=pltpu.VMEM)
    small = pl.BlockSpec(memory_space=pltpu.SMEM)
    return pl.pallas_call(
        combine_kernel,
        in_specs=[small, small, whole, whole] + [pl.BlockSpec(memory_space=pl.ANY)] * len(after),
        out_specs=whole,
        out_shape=jax.ShapeDtypeStruct((number,) + own.shape[1:], jnp.float32),
        compiler_params=pltpu.CompilerParams(vmem_limit_bytes=VMEM),
        cost_estimate=QUICK,
        name="combine",
    )(me, factors, own, far, *after)


def inner_kernel(count, me, factors, cos_high, cos_low, sin_high, sin_low, *rest):
    out, token = rest[-2:]
    y_re = y_im = 0.0
    for i, block in enumerate(rest[:count]):
        f_re, f_im = (factors[0, :, 2 * i + j : 2 * i + j + 1] for j in range(2))
        y_re += f_re * block[0]
        y_im += f_im * block[0]
        if block.shape[0] == 2:
            y_re -= f_im * block[1]
            y_im += f_re * block[1]
    both = split_bf16(jnp.concatenate([y_re, y_im], axis=1))
    cos_part = dot3((cos_high[...], cos_low[...]), both)
    sin_part = dot3((sin_high[...], sin_low[...]), both)
    out[0] = cos_part[:, :LANES] + sin_part[:, LANES:]
    out[1] = cos_part[:, LANES:] - sin_part[:, :LANES]
    token[...] = jnp.zeros_like(token)


def inner(me, factors, tables, blocks, result, block, full_width, after):
    number, rows, width = blocks[0].shape
    kept = [] if result is None else [result]
    inputs = [me, factors, *tables, *blocks, *after, *kept]
    specs = (
        [pl.BlockSpec((1,) + factors.shape[1:], lambda i, at: (at[0], 0, 0))]
        + [pl.BlockSpec((rows, rows), lambda i, at: (0, 0))] * 4
        + [pl.BlockSpec((number, rows, LANES), lambda i, at: (0, 0, i))] * len(blocks)
        + [pl.BlockSpec(memory_space=pl.ANY)] * (len(after) + len(kept))
    )
    return pl.pallas_call(
        functools.partial(inner_kernel, len(blocks)),
        grid_spec=pltpu.PrefetchScalarGridSpec(
            num_scalar_prefetch=1,
            grid=(width // LANES,),
            in_specs=specs,
            out_specs=[
                pl.BlockSpec((2, rows, LANES), lambda i, at: (0, 0, block + i)),
                pl.BlockSpec((8, LANES), lambda i, at: (0, 0)),
            ],
        ),
        out_shape=[
            jax.ShapeDtypeStruct((2, rows, full_width), jnp.float32),
            jax.ShapeDtypeStruct((8, LANES), jnp.float32),
        ],
        input_output_aliases={len(inputs) - 1: 0} if kept else {},
        compiler_params=pltpu.CompilerParams(vmem_limit_bytes=VMEM),
        cost_estimate=QUICK,
        name="inner",
    )(*inputs)


def column_chunks(count):
    chunks, at = [], 1
    while at < count - 1:
        size = SIZES[min(len(chunks), len(SIZES) - 1)]
        chunks.append((at, min(size, count - 1 - at)))
        at += size
    return chunks + [(0, 1), (count - 1, 1)]


def reversed_bits(value, levels):
    return sum((value >> i & 1) << levels - 1 - i for i in range(levels))


def butterfly_plan(devices):
    stages = []
    phase = np.ones(devices, np.complex128)
    is_real = [True] * devices
    half = devices // 2
    while half:
        own, far = np.zeros(devices, np.complex128), np.zeros(devices, np.complex128)
        next_phase, next_real = phase.copy(), list(is_real)
        for a in range(devices):
            b = a ^ half
            upper = bool(a & half)
            turn = np.exp(-2j * np.pi * (a % half) / (2 * half)) if upper else 1.0
            keep = is_real[a] and phase[a] == 1 and phase[b] == 1
            if keep:
                own[a], far[a] = (-1 if upper else 1), 1
                next_phase[a] = turn
            else:
                own[a] = phase[a] * (-turn if upper else 1)
                far[a] = phase[b] * turn
                next_phase[a], next_real[a] = 1, False
        stages.append((half, own, far, [a for a in range(devices) if not is_real[a]], next_phase))
        phase, is_real = next_phase, next_real
        half //= 2
    return stages


def inner_tables(count, total):
    index = np.arange(count)
    angle = 2 * np.pi / count * (index[:, None] * index[None, :] % count)
    tables = []
    for part in (np.cos(angle), np.sin(angle)):
        part = part / math.sqrt(total)
        high = part.astype(jnp.bfloat16)
        tables += [high, (part - high.astype(np.float64)).astype(jnp.bfloat16)]
    return [jnp.asarray(t) for t in tables]


def parts(*values):
    return np.stack([p for v in values for p in (v.real, v.imag)], -1).astype(np.float32)


def on_device(signal, apod, coef, block_offset, fine_start):
    rows, width = signal.shape
    devices = lax.axis_size("row")
    me = lax.axis_index("row").astype(jnp.int32)[None]
    levels = devices.bit_length() - 1
    total = rows * devices
    count = width // LANES

    neighbours = lax.axis_size("col")
    up = [(i, i + 1) for i in range(neighbours - 1)]
    down = [(j, i) for i, j in up]
    before = lax.ppermute(signal[:, width - LANES :], "col", up)
    behind = lax.ppermute(signal[:, :LANES], "col", down)

    stages = butterfly_plan(devices)
    tables = inner_tables(rows, total)
    outer = np.array([reversed_bits(a, levels) for a in range(devices)])
    twiddle = np.exp(-2j * np.pi / total * (outer[:, None] * np.arange(rows)[None, :] % total))
    factors = [jnp.asarray(parts(own, far)) for _, own, far, _, _ in stages[:-1]]
    _, own, far, _, phase = stages[-1]
    own, far = (own * phase)[:, None] * twiddle, (far * phase)[:, None] * twiddle
    factors.append(jnp.asarray(parts(own, far)))
    half, near_own, near_far = stages[-2][:3]
    flip = np.arange(devices) ^ stages[-1][0]
    direct = [own * near_own[:, None], own * near_far[:, None]]
    direct += [far * near_own[flip, None], far * near_far[flip, None]]
    partners = [half, stages[-1][0], half ^ stages[-1][0]]
    factors.append(jnp.asarray(parts(*direct)))
    numbers = [2 if stages[s + 1][3] else 1 for s in range(levels - 1)]

    chunks = column_chunks(count)

    def send(value, half):
        return lax.ppermute(value, "row", [(a, a ^ half) for a in range(devices)])

    out, far, results = {}, {}, {}
    stage_of = {"stencil": 0, "first": 1, "middle": levels - 1, "inner": levels}

    def is_direct(chunk):
        return chunk >= len(chunks) - DIRECT

    def after(name, chunk):
        kept = []
        for what, shift in ORDER[name]:
            at = chunk + shift
            if 0 <= at < len(chunks):
                if what == "arrived":
                    make(0, at)
                    kept.append(far[0, at][0])
                elif stage_of[what] != levels - 1 or not is_direct(at):
                    make(stage_of[what], at)
                    kept.append(out[stage_of[what], at])
        return kept

    def make(stage, chunk):
        if (stage, chunk) in out:
            return
        block, number = chunks[chunk]
        if stage == 0:
            left = (before, 0) if block == 0 else (signal, block - 1)
            right = (behind, 0) if block == count - 1 else (signal, block + 1)
            out[stage, chunk] = stencil(
                left,
                (signal, block),
                right,
                apod[None, :],
                coef,
                fine_start[None, :],
                block_offset,
                block,
                number,
                after("stencil", chunk),
                VMEM if chunk else FIRST_VMEM,
            )
            waits = after("gate", chunk)
            if waits:
                out[stage, chunk] = gate(out[stage, chunk], waits)
        else:
            source = levels - 2 if stage == levels and is_direct(chunk) else stage - 1
            make(source, chunk)
            near, there = out[source, chunk], far[source, chunk]
            if stage < levels:
                out[stage, chunk] = combine(
                    me,
                    factors[stage - 1],
                    near,
                    there[0],
                    numbers[stage - 1],
                    after("first" if stage == 1 else "middle", chunk),
                )
            else:
                if chunk:
                    make(stage, chunk - 1)
                results[chunk], out[stage, chunk] = inner(
                    me,
                    factors[len(there) // 2 + levels - 1],
                    tables,
                    [near, *there],
                    results.get(chunk - 1),
                    block,
                    width,
                    after("inner", chunk),
                )
        if stage < levels:
            ways = partners if stage == levels - 2 and is_direct(chunk) else [stages[stage][0]]
            far[stage, chunk] = [send(out[stage, chunk], half) for half in ways]

    make(levels, len(chunks) - 1)
    return results[len(chunks) - 1]


def solution(mesh):
    placed = (P("row", "col"), P("row"), P(None, "col"), P("col"), P("col"))
    return jax.shard_map(
        on_device, mesh=mesh, in_specs=placed, out_specs=P(None, "row", "col"), check_vma=False
    )
```

```python
import functools
import math

import jax
import jax.numpy as jnp
import numpy as np
from jax import lax
from jax.experimental import pallas as pl
from jax.experimental.pallas import tpu as pltpu
from jax.sharding import PartitionSpec as P

TAPS = 4
LANES = 128
DIRECT = (-1,)
SIZES = (1, 1, 1, 1, 1, 1)
ORDER = {'stencil': [], 'gate': [('arrived', -1)], 'first': [('inner', -3), ('middle', -1)], 'middle': [('stencil', 2), ('inner', -2)], 'inner': [('middle', 1)]}
MIB = 1024 * 1024
VMEM = 20 * MIB
GATE_VMEM = 1 * MIB
FIRST_VMEM = 56 * MIB
QUICK = pl.CostEstimate(flops=0, bytes_accessed=0, transcendentals=0)


def split_bf16(value):
    high = value.astype(jnp.bfloat16)
    low = (value - high.astype(jnp.float32)).astype(jnp.bfloat16)
    return high, low


def dot3(a, b):
    dot = functools.partial(jnp.dot, preferred_element_type=jnp.float32)
    return dot(a[0], b[0]) + (dot(a[0], b[1]) + dot(a[1], b[0]))


def stencil_kernel(first, per_block, offsets, left, mid, right, apod, coef, fine, *rest):
    out = rest[-1]
    rows = mid.shape[0]
    block = first + pl.program_id(0)
    lane = lax.broadcasted_iota(jnp.int32, (1, LANES), 1)
    start = fine[...]
    if per_block >= LANES:
        start = start + offsets[block * LANES // per_block]
    else:
        for part in range(LANES // per_block):
            value = offsets[block * (LANES // per_block) + part]
            start = start + jnp.where(lane // per_block == part, value, 0)
    shape = (3 * LANES, LANES)
    tap_at = (
        lax.broadcasted_iota(jnp.int32, shape, 0)
        - lax.broadcasted_iota(jnp.int32, shape, 1)
        - LANES
        - start
    )
    band = jnp.zeros(shape, jnp.float32)
    for tap in range(TAPS):
        band = jnp.where(tap_at == tap, coef[tap : tap + 1, :], band)
    field = jnp.concatenate([left[...], mid[...], right[...]], axis=1)
    window = jnp.broadcast_to(apod[...], (LANES, rows)).T
    out[...] = window * dot3(split_bf16(field), split_bf16(band))


def stencil(left, mid, right, apod, coef, fine, offsets, block, count, after, vmem=VMEM):
    rows, width = mid[0].shape

    def columns(height, at):
        return pl.BlockSpec((height, LANES), lambda i: (0, at + i))

    return pl.pallas_call(
        functools.partial(stencil_kernel, block, width // offsets.shape[0]),
        grid=(count,),
        in_specs=[pl.BlockSpec(memory_space=pltpu.SMEM)]
        + [columns(rows, at) for _, at in (left, mid, right)]
        + [
            pl.BlockSpec((1, rows), lambda i: (0, 0)),
            columns(TAPS, block),
            columns(1, block),
        ]
        + [pl.BlockSpec(memory_space=pl.ANY)] * len(after),
        out_specs=pl.BlockSpec((rows, LANES), lambda i: (0, i)),
        out_shape=jax.ShapeDtypeStruct((rows, count * LANES), jnp.float32),
        compiler_params=pltpu.CompilerParams(vmem_limit_bytes=vmem),
        cost_estimate=QUICK,
        name="stencil",
    )(offsets, left[0], mid[0], right[0], apod, coef, fine, *after)


def gate_kernel(value, *rest):
    pass


def gate(value, after):
    anywhere = pl.BlockSpec(memory_space=pl.ANY)
    return pl.pallas_call(
        gate_kernel,
        in_specs=[anywhere] * (1 + len(after)),
        out_specs=anywhere,
        out_shape=jax.ShapeDtypeStruct(value.shape, value.dtype),
        input_output_aliases={0: 0},
        compiler_params=pltpu.CompilerParams(vmem_limit_bytes=GATE_VMEM),
        cost_estimate=QUICK,
        name="gate",
    )(value, *after)


def combine_kernel(parts_in, parts_out, me, factors, *refs):
    own, far, out = refs[:parts_in], refs[parts_in : 2 * parts_in], refs[-parts_out:]
    a_re, a_im, b_re, b_im = (factors[me[0], i] for i in range(4))
    real = a_re * own[0][...] + b_re * far[0][...]
    if parts_in == 2:
        real -= a_im * own[1][...] + b_im * far[1][...]
    out[0][...] = real
    if parts_out == 2:
        imag = a_im * own[0][...] + b_im * far[0][...]
        if parts_in == 2:
            imag += a_re * own[1][...] + b_re * far[1][...]
        out[1][...] = imag


def combine(me, factors, own, far, number, after):
    whole = pl.BlockSpec(memory_space=pltpu.VMEM)
    small = pl.BlockSpec(memory_space=pltpu.SMEM)
    return pl.pallas_call(
        functools.partial(combine_kernel, len(own), number),
        in_specs=[small, small]
        + [whole] * (2 * len(own))
        + [pl.BlockSpec(memory_space=pl.ANY)] * len(after),
        out_specs=[whole] * number,
        out_shape=[jax.ShapeDtypeStruct(own[0].shape, jnp.float32)] * number,
        compiler_params=pltpu.CompilerParams(vmem_limit_bytes=VMEM),
        cost_estimate=QUICK,
        name="combine",
    )(me, factors, *own, *far, *after)


def inner_kernel(count, me, factors, cos_high, cos_low, sin_high, sin_low, *rest):
    out, token = rest[-2:]
    y_re = y_im = 0.0
    for i, block in enumerate(rest[:count]):
        f_re, f_im = (factors[0, :, 2 * i + j : 2 * i + j + 1] for j in range(2))
        y_re += f_re * block[...]
        y_im += f_im * block[...]
    both = split_bf16(jnp.concatenate([y_re, y_im], axis=1))
    cos_part = dot3((cos_high[...], cos_low[...]), both)
    sin_part = dot3((sin_high[...], sin_low[...]), both)
    out[0] = cos_part[:, :LANES] + sin_part[:, LANES:]
    out[1] = cos_part[:, LANES:] - sin_part[:, :LANES]
    token[...] = jnp.zeros_like(token)


def inner(me, factors, tables, blocks, result, block, full_width, after):
    rows, width = blocks[0].shape
    kept = [] if result is None else [result]
    inputs = [me, factors, *tables, *blocks, *after, *kept]
    specs = (
        [pl.BlockSpec((1,) + factors.shape[1:], lambda i, at: (at[0], 0, 0))]
        + [pl.BlockSpec((rows, rows), lambda i, at: (0, 0))] * 4
        + [pl.BlockSpec((rows, LANES), lambda i, at: (0, i))] * len(blocks)
        + [pl.BlockSpec(memory_space=pl.ANY)] * (len(after) + len(kept))
    )
    return pl.pallas_call(
        functools.partial(inner_kernel, len(blocks)),
        grid_spec=pltpu.PrefetchScalarGridSpec(
            num_scalar_prefetch=1,
            grid=(width // LANES,),
            in_specs=specs,
            out_specs=[
                pl.BlockSpec((2, rows, LANES), lambda i, at: (0, 0, block + i)),
                pl.BlockSpec((8, LANES), lambda i, at: (0, 0)),
            ],
        ),
        out_shape=[
            jax.ShapeDtypeStruct((2, rows, full_width), jnp.float32),
            jax.ShapeDtypeStruct((8, LANES), jnp.float32),
        ],
        input_output_aliases={len(inputs) - 1: 0} if kept else {},
        compiler_params=pltpu.CompilerParams(vmem_limit_bytes=VMEM),
        cost_estimate=QUICK,
        name="inner",
    )(*inputs)


def column_chunks(count):
    chunks, at = [], 1
    while at < count - 1:
        size = SIZES[min(len(chunks), len(SIZES) - 1)]
        chunks.append((at, min(size, count - 1 - at)))
        at += size
    return chunks + [(0, 1), (count - 1, 1)]


def reversed_bits(value, levels):
    return sum((value >> i & 1) << levels - 1 - i for i in range(levels))


def butterfly_plan(devices):
    stages = []
    phase = np.ones(devices, np.complex128)
    is_real = [True] * devices
    half = devices // 2
    while half:
        own, far = np.zeros(devices, np.complex128), np.zeros(devices, np.complex128)
        next_phase, next_real = phase.copy(), list(is_real)
        for a in range(devices):
            b = a ^ half
            upper = bool(a & half)
            turn = np.exp(-2j * np.pi * (a % half) / (2 * half)) if upper else 1.0
            keep = is_real[a] and phase[a] == 1 and phase[b] == 1
            if keep:
                own[a], far[a] = (-1 if upper else 1), 1
                next_phase[a] = turn
            else:
                own[a] = phase[a] * (-turn if upper else 1)
                far[a] = phase[b] * turn
                next_phase[a], next_real[a] = 1, False
        stages.append((half, own, far, [a for a in range(devices) if not is_real[a]], next_phase))
        phase, is_real = next_phase, next_real
        half //= 2
    return stages


def inner_tables(count, total):
    index = np.arange(count)
    angle = 2 * np.pi / count * (index[:, None] * index[None, :] % count)
    tables = []
    for part in (np.cos(angle), np.sin(angle)):
        part = part / math.sqrt(total)
        high = part.astype(jnp.bfloat16)
        tables += [high, (part - high.astype(np.float64)).astype(jnp.bfloat16)]
    return [jnp.asarray(t) for t in tables]


def parts(*values):
    return np.stack([p for v in values for p in (v.real, v.imag)], -1).astype(np.float32)


def on_device(signal, apod, coef, block_offset, fine_start):
    rows, width = signal.shape
    devices = lax.axis_size("row")
    me = lax.axis_index("row").astype(jnp.int32)[None]
    levels = devices.bit_length() - 1
    total = rows * devices
    count = width // LANES

    neighbours = lax.axis_size("col")
    up = [(i, i + 1) for i in range(neighbours - 1)]
    down = [(j, i) for i, j in up]
    before = lax.ppermute(signal[:, width - LANES :], "col", up)
    behind = lax.ppermute(signal[:, :LANES], "col", down)

    stages = butterfly_plan(devices)
    tables = inner_tables(rows, total)
    outer = np.array([reversed_bits(a, levels) for a in range(devices)])
    twiddle = np.exp(-2j * np.pi / total * (outer[:, None] * np.arange(rows)[None, :] % total))
    factors = [jnp.asarray(parts(own, far)) for _, own, far, _, _ in stages[:-1]]
    _, own, far, _, phase = stages[-1]
    own, far = (own * phase)[:, None] * twiddle, (far * phase)[:, None] * twiddle
    numbers = [1] + [2 if stages[s + 1][3] else 1 for s in range(levels - 1)]

    def by_part(values, number):
        return jnp.asarray(parts(*(v * 1j**i for v in values for i in range(number))))

    factors.append(by_part([own, far], numbers[levels - 1]))
    half, near_own, near_far = stages[-2][:3]
    flip = np.arange(devices) ^ stages[-1][0]
    direct = [own * near_own[:, None], own * near_far[:, None]]
    direct += [far * near_own[flip, None], far * near_far[flip, None]]
    partners = [half, stages[-1][0], half ^ stages[-1][0]]
    factors.append(by_part(direct, numbers[levels - 2]))
    chunks = column_chunks(count)

    def send(values, half, stage):
        groups = [range(devices), stages[stage][3]]
        return [
            lax.ppermute(value, "row", [(a, a ^ half) for a in group])
            for value, group in zip(values, groups)
        ]

    out, far, results = {}, {}, {}
    stage_of = {"stencil": 0, "first": 1, "middle": levels - 1, "inner": levels}

    def is_direct(chunk):
        return chunk in DIRECT or chunk - len(chunks) in DIRECT

    def after(name, chunk):
        kept = []
        for what, shift in ORDER[name]:
            at = chunk + shift
            if 0 <= at < len(chunks):
                if what == "arrived":
                    make(0, at)
                    kept += far[0, at][0]
                elif stage_of[what] != levels - 1 or not is_direct(at):
                    make(stage_of[what], at)
                    kept += out[stage_of[what], at][-1:]
        return kept

    def make(stage, chunk):
        if (stage, chunk) in out:
            return
        block, number = chunks[chunk]
        if stage == 0:
            left = (before, 0) if block == 0 else (signal, block - 1)
            right = (behind, 0) if block == count - 1 else (signal, block + 1)
            field = stencil(
                left,
                (signal, block),
                right,
                apod[None, :],
                coef,
                fine_start[None, :],
                block_offset,
                block,
                number,
                after("stencil", chunk),
                VMEM if chunk else FIRST_VMEM,
            )
            waits = after("gate", chunk)
            out[stage, chunk] = [gate(field, waits) if waits else field]
        else:
            source = levels - 2 if stage == levels and is_direct(chunk) else stage - 1
            make(source, chunk)
            near, there = out[source, chunk], far[source, chunk]
            if stage < levels:
                out[stage, chunk] = combine(
                    me,
                    factors[stage - 1],
                    near,
                    there[0],
                    numbers[stage],
                    after("first" if stage == 1 else "middle", chunk),
                )
            else:
                if chunk:
                    make(stage, chunk - 1)
                results[chunk], token = inner(
                    me,
                    factors[len(there) // 2 + levels - 1],
                    tables,
                    [part for group in (near, *there) for part in group],
                    results.get(chunk - 1),
                    block,
                    width,
                    after("inner", chunk),
                )
                out[stage, chunk] = [token]
        if stage < levels:
            ways = partners if stage == levels - 2 and is_direct(chunk) else [stages[stage][0]]
            far[stage, chunk] = [send(out[stage, chunk], half, stage) for half in ways]

    make(levels, len(chunks) - 1)
    return results[len(chunks) - 1]


def solution(mesh):
    placed = (P("row", "col"), P("row"), P(None, "col"), P("col"), P("col"))
    return jax.shard_map(
        on_device, mesh=mesh, in_specs=placed, out_specs=P(None, "row", "col"), check_vma=False
    )
```

```python
import functools
import math

import jax
import jax.numpy as jnp
import numpy as np
from jax import lax
from jax.experimental import pallas as pl
from jax.experimental.pallas import tpu as pltpu
from jax.sharding import PartitionSpec as P

TAPS = 4
LANES = 128
DIRECT = 2
SIZES = (1, 1, 1, 1, 1, 1)
ORDER = {'stencil': [], 'gate': [('arrived', -1)], 'first': [('inner', -3), ('middle', -1)], 'middle': [('stencil', 2)], 'inner': [('middle', 1)]}
MIB = 1024 * 1024
VMEM = 20 * MIB
GATE_VMEM = 1 * MIB
FIRST_VMEM = 56 * MIB
QUICK = pl.CostEstimate(flops=0, bytes_accessed=0, transcendentals=0)


def split_bf16(value):
    high = value.astype(jnp.bfloat16)
    low = (value - high.astype(jnp.float32)).astype(jnp.bfloat16)
    return high, low


def dot3(a, b):
    dot = functools.partial(jnp.dot, preferred_element_type=jnp.float32)
    return dot(a[0], b[0]) + (dot(a[0], b[1]) + dot(a[1], b[0]))


def stencil_kernel(first, per_block, offsets, left, mid, right, apod, coef, fine, *rest):
    out = rest[-1]
    rows = mid.shape[0]
    block = first + pl.program_id(0)
    lane = lax.broadcasted_iota(jnp.int32, (1, LANES), 1)
    start = fine[...]
    if per_block >= LANES:
        start = start + offsets[block * LANES // per_block]
    else:
        for part in range(LANES // per_block):
            value = offsets[block * (LANES // per_block) + part]
            start = start + jnp.where(lane // per_block == part, value, 0)
    shape = (3 * LANES, LANES)
    tap_at = (
        lax.broadcasted_iota(jnp.int32, shape, 0)
        - lax.broadcasted_iota(jnp.int32, shape, 1)
        - LANES
        - start
    )
    band = jnp.zeros(shape, jnp.float32)
    for tap in range(TAPS):
        band = jnp.where(tap_at == tap, coef[tap : tap + 1, :], band)
    field = jnp.concatenate([left[...], mid[...], right[...]], axis=1)
    window = jnp.broadcast_to(apod[...], (LANES, rows)).T
    out[0] = window * dot3(split_bf16(field), split_bf16(band))


def stencil(left, mid, right, apod, coef, fine, offsets, block, count, after, vmem=VMEM):
    rows, width = mid[0].shape

    def columns(height, at):
        return pl.BlockSpec((height, LANES), lambda i: (0, at + i))

    return pl.pallas_call(
        functools.partial(stencil_kernel, block, width // offsets.shape[0]),
        grid=(count,),
        in_specs=[pl.BlockSpec(memory_space=pltpu.SMEM)]
        + [columns(rows, at) for _, at in (left, mid, right)]
        + [
            pl.BlockSpec((1, rows), lambda i: (0, 0)),
            columns(TAPS, block),
            columns(1, block),
        ]
        + [pl.BlockSpec(memory_space=pl.ANY)] * len(after),
        out_specs=pl.BlockSpec((1, rows, LANES), lambda i: (0, 0, i)),
        out_shape=jax.ShapeDtypeStruct((1, rows, count * LANES), jnp.float32),
        compiler_params=pltpu.CompilerParams(vmem_limit_bytes=vmem),
        cost_estimate=QUICK,
        name="stencil",
    )(offsets, left[0], mid[0], right[0], apod, coef, fine, *after)


def gate_kernel(value, *rest):
    pass


def gate(value, after):
    anywhere = pl.BlockSpec(memory_space=pl.ANY)
    return pl.pallas_call(
        gate_kernel,
        in_specs=[anywhere] * (1 + len(after)),
        out_specs=anywhere,
        out_shape=jax.ShapeDtypeStruct(value.shape, value.dtype),
        input_output_aliases={0: 0},
        compiler_params=pltpu.CompilerParams(vmem_limit_bytes=GATE_VMEM),
        cost_estimate=QUICK,
        name="gate",
    )(value, *after)


def combine_kernel(me, factors, own, far, *rest):
    out = rest[-1]
    a_re, a_im, b_re, b_im = (factors[me[0], i] for i in range(4))
    if own.shape[0] == 2:
        out[0] = a_re * own[0] - a_im * own[1] + (b_re * far[0] - b_im * far[1])
        out[1] = a_re * own[1] + a_im * own[0] + (b_re * far[1] + b_im * far[0])
    elif out.shape[0] == 2:
        out[0] = a_re * own[0] + b_re * far[0]
        out[1] = a_im * own[0] + b_im * far[0]
    else:
        out[0] = a_re * own[0] + b_re * far[0]


def combine(me, factors, own, far, number, after):
    whole = pl.BlockSpec(memory_space=pltpu.VMEM)
    small = pl.BlockSpec(memory_space=pltpu.SMEM)
    return pl.pallas_call(
        combine_kernel,
        in_specs=[small, small, whole, whole] + [pl.BlockSpec(memory_space=pl.ANY)] * len(after),
        out_specs=whole,
        out_shape=jax.ShapeDtypeStruct((number,) + own.shape[1:], jnp.float32),
        compiler_params=pltpu.CompilerParams(vmem_limit_bytes=VMEM),
        cost_estimate=QUICK,
        name="combine",
    )(me, factors, own, far, *after)


def inner_kernel(count, me, factors, cos_high, cos_low, sin_high, sin_low, *rest):
    out, token = rest[-2:]
    y_re = y_im = 0.0
    for i, block in enumerate(rest[:count]):
        f_re, f_im = (factors[0, :, 2 * i + j : 2 * i + j + 1] for j in range(2))
        y_re += f_re * block[0]
        y_im += f_im * block[0]
        if block.shape[0] == 2:
            y_re -= f_im * block[1]
            y_im += f_re * block[1]
    both = split_bf16(jnp.concatenate([y_re, y_im], axis=1))
    cos_part = dot3((cos_high[...], cos_low[...]), both)
    sin_part = dot3((sin_high[...], sin_low[...]), both)
    out[0] = cos_part[:, :LANES] + sin_part[:, LANES:]
    out[1] = cos_part[:, LANES:] - sin_part[:, :LANES]
    token[...] = jnp.zeros_like(token)


def inner(me, factors, tables, blocks, result, block, full_width, after):
    number, rows, width = blocks[0].shape
    kept = [] if result is None else [result]
    inputs = [me, factors, *tables, *blocks, *after, *kept]
    specs = (
        [pl.BlockSpec((1,) + factors.shape[1:], lambda i, at: (at[0], 0, 0))]
        + [pl.BlockSpec((rows, rows), lambda i, at: (0, 0))] * 4
        + [pl.BlockSpec((number, rows, LANES), lambda i, at: (0, 0, i))] * len(blocks)
        + [pl.BlockSpec(memory_space=pl.ANY)] * (len(after) + len(kept))
    )
    return pl.pallas_call(
        functools.partial(inner_kernel, len(blocks)),
        grid_spec=pltpu.PrefetchScalarGridSpec(
            num_scalar_prefetch=1,
            grid=(width // LANES,),
            in_specs=specs,
            out_specs=[
                pl.BlockSpec((2, rows, LANES), lambda i, at: (0, 0, block + i)),
                pl.BlockSpec((8, LANES), lambda i, at: (0, 0)),
            ],
        ),
        out_shape=[
            jax.ShapeDtypeStruct((2, rows, full_width), jnp.float32),
            jax.ShapeDtypeStruct((8, LANES), jnp.float32),
        ],
        input_output_aliases={len(inputs) - 1: 0} if kept else {},
        compiler_params=pltpu.CompilerParams(vmem_limit_bytes=VMEM),
        cost_estimate=QUICK,
        name="inner",
    )(*inputs)


def column_chunks(count):
    chunks, at = [], 1
    while at < count - 1:
        size = SIZES[min(len(chunks), len(SIZES) - 1)]
        chunks.append((at, min(size, count - 1 - at)))
        at += size
    return chunks + [(0, 1), (count - 1, 1)]


def reversed_bits(value, levels):
    return sum((value >> i & 1) << levels - 1 - i for i in range(levels))


def butterfly_plan(devices):
    stages = []
    phase = np.ones(devices, np.complex128)
    is_real = [True] * devices
    half = devices // 2
    while half:
        own, far = np.zeros(devices, np.complex128), np.zeros(devices, np.complex128)
        next_phase, next_real = phase.copy(), list(is_real)
        for a in range(devices):
            b = a ^ half
            upper = bool(a & half)
            turn = np.exp(-2j * np.pi * (a % half) / (2 * half)) if upper else 1.0
            keep = is_real[a] and phase[a] == 1 and phase[b] == 1
            if keep:
                own[a], far[a] = (-1 if upper else 1), 1
                next_phase[a] = turn
            else:
                own[a] = phase[a] * (-turn if upper else 1)
                far[a] = phase[b] * turn
                next_phase[a], next_real[a] = 1, False
        stages.append((half, own, far, [a for a in range(devices) if not is_real[a]], next_phase))
        phase, is_real = next_phase, next_real
        half //= 2
    return stages


def inner_tables(count, total):
    index = np.arange(count)
    angle = 2 * np.pi / count * (index[:, None] * index[None, :] % count)
    tables = []
    for part in (np.cos(angle), np.sin(angle)):
        part = part / math.sqrt(total)
        high = part.astype(jnp.bfloat16)
        tables += [high, (part - high.astype(np.float64)).astype(jnp.bfloat16)]
    return [jnp.asarray(t) for t in tables]


def parts(*values):
    return np.stack([p for v in values for p in (v.real, v.imag)], -1).astype(np.float32)


def on_device(signal, apod, coef, block_offset, fine_start):
    rows, width = signal.shape
    devices = lax.axis_size("row")
    me = lax.axis_index("row").astype(jnp.int32)[None]
    levels = devices.bit_length() - 1
    total = rows * devices
    count = width // LANES

    neighbours = lax.axis_size("col")
    up = [(i, i + 1) for i in range(neighbours - 1)]
    down = [(j, i) for i, j in up]
    before = lax.ppermute(signal[:, width - LANES :], "col", up)
    behind = lax.ppermute(signal[:, :LANES], "col", down)

    stages = butterfly_plan(devices)
    tables = inner_tables(rows, total)
    outer = np.array([reversed_bits(a, levels) for a in range(devices)])
    twiddle = np.exp(-2j * np.pi / total * (outer[:, None] * np.arange(rows)[None, :] % total))
    factors = [jnp.asarray(parts(own, far)) for _, own, far, _, _ in stages[:-1]]
    _, own, far, _, phase = stages[-1]
    own, far = (own * phase)[:, None] * twiddle, (far * phase)[:, None] * twiddle
    factors.append(jnp.asarray(parts(own, far)))
    half, near_own, near_far = stages[-2][:3]
    flip = np.arange(devices) ^ stages[-1][0]
    direct = [own * near_own[:, None], own * near_far[:, None]]
    direct += [far * near_own[flip, None], far * near_far[flip, None]]
    partners = [half, stages[-1][0], half ^ stages[-1][0]]
    factors.append(jnp.asarray(parts(*direct)))
    numbers = [2 if stages[s + 1][3] else 1 for s in range(levels - 1)]

    chunks = column_chunks(count)

    def send(value, half):
        return lax.ppermute(value, "row", [(a, a ^ half) for a in range(devices)])

    out, far, results = {}, {}, {}
    stage_of = {"stencil": 0, "first": 1, "middle": levels - 1, "inner": levels}

    def is_direct(chunk):
        return chunk >= len(chunks) - DIRECT

    def after(name, chunk):
        kept = []
        for what, shift in ORDER[name]:
            at = chunk + shift
            if 0 <= at < len(chunks):
                if what == "arrived":
                    make(0, at)
                    kept.append(far[0, at][0])
                elif stage_of[what] != levels - 1 or not is_direct(at):
                    make(stage_of[what], at)
                    kept.append(out[stage_of[what], at])
        return kept

    def make(stage, chunk):
        if (stage, chunk) in out:
            return
        block, number = chunks[chunk]
        if stage == 0:
            left = (before, 0) if block == 0 else (signal, block - 1)
            right = (behind, 0) if block == count - 1 else (signal, block + 1)
            out[stage, chunk] = stencil(
                left,
                (signal, block),
                right,
                apod[None, :],
                coef,
                fine_start[None, :],
                block_offset,
                block,
                number,
                after("stencil", chunk),
                VMEM if chunk else FIRST_VMEM,
            )
            waits = after("gate", chunk)
            if waits:
                out[stage, chunk] = gate(out[stage, chunk], waits)
        else:
            source = levels - 2 if stage == levels and is_direct(chunk) else stage - 1
            make(source, chunk)
            near, there = out[source, chunk], far[source, chunk]
            if stage < levels:
                out[stage, chunk] = combine(
                    me,
                    factors[stage - 1],
                    near,
                    there[0],
                    numbers[stage - 1],
                    after("first" if stage == 1 else "middle", chunk),
                )
            else:
                if chunk:
                    make(stage, chunk - 1)
                results[chunk], out[stage, chunk] = inner(
                    me,
                    factors[len(there) // 2 + levels - 1],
                    tables,
                    [near, *there],
                    results.get(chunk - 1),
                    block,
                    width,
                    after("inner", chunk),
                )
        if stage < levels:
            ways = partners if stage == levels - 2 and is_direct(chunk) else [stages[stage][0]]
            far[stage, chunk] = [send(out[stage, chunk], half) for half in ways]

    make(levels, len(chunks) - 1)
    return results[len(chunks) - 1]


def solution(mesh):
    placed = (P("row", "col"), P("row"), P(None, "col"), P("col"), P("col"))
    return jax.shard_map(
        on_device, mesh=mesh, in_specs=placed, out_specs=P(None, "row", "col"), check_vma=False
    )
```

```python
import functools
import math

import jax
import jax.numpy as jnp
import numpy as np
from jax import lax
from jax.experimental import pallas as pl
from jax.experimental.pallas import tpu as pltpu
from jax.sharding import PartitionSpec as P

TAPS = 4
LANES = 128
DIRECT = 1
SIZES = (1, 1, 1, 1, 1, 1)
ORDER = {
    "stencil": [],
    "gate": [("arrived", -1)],
    "first": [("inner", -3)],
    "middle": [("stencil", 2), ("inner", -2)],
    "inner": [],
}
MIB = 1024 * 1024
VMEM = 20 * MIB
GATE_VMEM = 1 * MIB
FIRST_VMEM = 56 * MIB
QUICK = pl.CostEstimate(flops=0, bytes_accessed=0, transcendentals=0)


def split_bf16(value):
    high = value.astype(jnp.bfloat16)
    low = (value - high.astype(jnp.float32)).astype(jnp.bfloat16)
    return high, low


def dot3(a, b):
    dot = functools.partial(jnp.dot, preferred_element_type=jnp.float32)
    return dot(a[0], b[0]) + (dot(a[0], b[1]) + dot(a[1], b[0]))


def stencil_kernel(first, per_block, offsets, left, mid, right, apod, coef, fine, *rest):
    out = rest[-1]
    rows = mid.shape[0]
    block = first + pl.program_id(0)
    lane = lax.broadcasted_iota(jnp.int32, (1, LANES), 1)
    start = fine[...]
    if per_block >= LANES:
        start = start + offsets[block * LANES // per_block]
    else:
        for part in range(LANES // per_block):
            value = offsets[block * (LANES // per_block) + part]
            start = start + jnp.where(lane // per_block == part, value, 0)
    shape = (3 * LANES, LANES)
    tap_at = (
        lax.broadcasted_iota(jnp.int32, shape, 0)
        - lax.broadcasted_iota(jnp.int32, shape, 1)
        - LANES
        - start
    )
    band = jnp.zeros(shape, jnp.float32)
    for tap in range(TAPS):
        band = jnp.where(tap_at == tap, coef[tap : tap + 1, :], band)
    field = jnp.concatenate([left[...], mid[...], right[...]], axis=1)
    window = jnp.broadcast_to(apod[...], (LANES, rows)).T
    out[0] = window * dot3(split_bf16(field), split_bf16(band))


def stencil(left, mid, right, apod, coef, fine, offsets, block, count, after, vmem=VMEM):
    rows, width = mid[0].shape

    def columns(height, at):
        return pl.BlockSpec((height, LANES), lambda i: (0, at + i))

    return pl.pallas_call(
        functools.partial(stencil_kernel, block, width // offsets.shape[0]),
        grid=(count,),
        in_specs=[pl.BlockSpec(memory_space=pltpu.SMEM)]
        + [columns(rows, at) for _, at in (left, mid, right)]
        + [
            pl.BlockSpec((1, rows), lambda i: (0, 0)),
            columns(TAPS, block),
            columns(1, block),
        ]
        + [pl.BlockSpec(memory_space=pl.ANY)] * len(after),
        out_specs=pl.BlockSpec((1, rows, LANES), lambda i: (0, 0, i)),
        out_shape=jax.ShapeDtypeStruct((1, rows, count * LANES), jnp.float32),
        compiler_params=pltpu.CompilerParams(vmem_limit_bytes=vmem),
        cost_estimate=QUICK,
        name="stencil",
    )(offsets, left[0], mid[0], right[0], apod, coef, fine, *after)


def gate_kernel(value, *rest):
    pass


def gate(value, after):
    anywhere = pl.BlockSpec(memory_space=pl.ANY)
    return pl.pallas_call(
        gate_kernel,
        in_specs=[anywhere] * (1 + len(after)),
        out_specs=anywhere,
        out_shape=jax.ShapeDtypeStruct(value.shape, value.dtype),
        input_output_aliases={0: 0},
        compiler_params=pltpu.CompilerParams(vmem_limit_bytes=GATE_VMEM),
        cost_estimate=QUICK,
        name="gate",
    )(value, *after)


def combine_kernel(me, factors, own, far, *rest):
    out = rest[-1]
    a_re, a_im, b_re, b_im = (factors[me[0], i] for i in range(4))
    if own.shape[0] == 2:
        out[0] = a_re * own[0] - a_im * own[1] + (b_re * far[0] - b_im * far[1])
        out[1] = a_re * own[1] + a_im * own[0] + (b_re * far[1] + b_im * far[0])
    elif out.shape[0] == 2:
        out[0] = a_re * own[0] + b_re * far[0]
        out[1] = a_im * own[0] + b_im * far[0]
    else:
        out[0] = a_re * own[0] + b_re * far[0]


def combine(me, factors, own, far, number, after):
    whole = pl.BlockSpec(memory_space=pltpu.VMEM)
    small = pl.BlockSpec(memory_space=pltpu.SMEM)
    return pl.pallas_call(
        combine_kernel,
        in_specs=[small, small, whole, whole] + [pl.BlockSpec(memory_space=pl.ANY)] * len(after),
        out_specs=whole,
        out_shape=jax.ShapeDtypeStruct((number,) + own.shape[1:], jnp.float32),
        compiler_params=pltpu.CompilerParams(vmem_limit_bytes=VMEM),
        cost_estimate=QUICK,
        name="combine",
    )(me, factors, own, far, *after)


def inner_kernel(count, me, factors, cos_high, cos_low, sin_high, sin_low, *rest):
    out, token = rest[-2:]
    y_re = y_im = 0.0
    for i, block in enumerate(rest[:count]):
        f_re, f_im = (factors[0, :, 2 * i + j : 2 * i + j + 1] for j in range(2))
        y_re += f_re * block[0]
        y_im += f_im * block[0]
        if block.shape[0] == 2:
            y_re -= f_im * block[1]
            y_im += f_re * block[1]
    both = split_bf16(jnp.concatenate([y_re, y_im], axis=1))
    cos_part = dot3((cos_high[...], cos_low[...]), both)
    sin_part = dot3((sin_high[...], sin_low[...]), both)
    out[0] = cos_part[:, :LANES] + sin_part[:, LANES:]
    out[1] = cos_part[:, LANES:] - sin_part[:, :LANES]
    token[...] = jnp.zeros_like(token)


def inner(me, factors, tables, blocks, result, block, full_width, after):
    number, rows, width = blocks[0].shape
    kept = [] if result is None else [result]
    inputs = [me, factors, *tables, *blocks, *after, *kept]
    specs = (
        [pl.BlockSpec((1,) + factors.shape[1:], lambda i, at: (at[0], 0, 0))]
        + [pl.BlockSpec((rows, rows), lambda i, at: (0, 0))] * 4
        + [pl.BlockSpec((number, rows, LANES), lambda i, at: (0, 0, i))] * len(blocks)
        + [pl.BlockSpec(memory_space=pl.ANY)] * (len(after) + len(kept))
    )
    return pl.pallas_call(
        functools.partial(inner_kernel, len(blocks)),
        grid_spec=pltpu.PrefetchScalarGridSpec(
            num_scalar_prefetch=1,
            grid=(width // LANES,),
            in_specs=specs,
            out_specs=[
                pl.BlockSpec((2, rows, LANES), lambda i, at: (0, 0, block + i)),
                pl.BlockSpec((8, LANES), lambda i, at: (0, 0)),
            ],
        ),
        out_shape=[
            jax.ShapeDtypeStruct((2, rows, full_width), jnp.float32),
            jax.ShapeDtypeStruct((8, LANES), jnp.float32),
        ],
        input_output_aliases={len(inputs) - 1: 0} if kept else {},
        compiler_params=pltpu.CompilerParams(vmem_limit_bytes=VMEM),
        cost_estimate=QUICK,
        name="inner",
    )(*inputs)


def column_chunks(count):
    chunks, at = [], 1
    while at < count - 1:
        size = SIZES[min(len(chunks), len(SIZES) - 1)]
        chunks.append((at, min(size, count - 1 - at)))
        at += size
    return chunks + [(0, 1), (count - 1, 1)]


def reversed_bits(value, levels):
    return sum((value >> i & 1) << levels - 1 - i for i in range(levels))


def butterfly_plan(devices):
    stages = []
    phase = np.ones(devices, np.complex128)
    is_real = [True] * devices
    half = devices // 2
    while half:
        own, far = np.zeros(devices, np.complex128), np.zeros(devices, np.complex128)
        next_phase, next_real = phase.copy(), list(is_real)
        for a in range(devices):
            b = a ^ half
            upper = bool(a & half)
            turn = np.exp(-2j * np.pi * (a % half) / (2 * half)) if upper else 1.0
            keep = is_real[a] and phase[a] == 1 and phase[b] == 1
            if keep:
                own[a], far[a] = (-1 if upper else 1), 1
                next_phase[a] = turn
            else:
                own[a] = phase[a] * (-turn if upper else 1)
                far[a] = phase[b] * turn
                next_phase[a], next_real[a] = 1, False
        stages.append((half, own, far, [a for a in range(devices) if not is_real[a]], next_phase))
        phase, is_real = next_phase, next_real
        half //= 2
    return stages


def inner_tables(count, total):
    index = np.arange(count)
    angle = 2 * np.pi / count * (index[:, None] * index[None, :] % count)
    tables = []
    for part in (np.cos(angle), np.sin(angle)):
        part = part / math.sqrt(total)
        high = part.astype(jnp.bfloat16)
        tables += [high, (part - high.astype(np.float64)).astype(jnp.bfloat16)]
    return [jnp.asarray(t) for t in tables]


def parts(*values):
    return np.stack([p for v in values for p in (v.real, v.imag)], -1).astype(np.float32)


def on_device(signal, apod, coef, block_offset, fine_start):
    rows, width = signal.shape
    devices = lax.axis_size("row")
    me = lax.axis_index("row").astype(jnp.int32)[None]
    levels = devices.bit_length() - 1
    total = rows * devices
    count = width // LANES

    neighbours = lax.axis_size("col")
    up = [(i, i + 1) for i in range(neighbours - 1)]
    down = [(j, i) for i, j in up]
    before = lax.ppermute(signal[:, width - LANES :], "col", up)
    behind = lax.ppermute(signal[:, :LANES], "col", down)

    stages = butterfly_plan(devices)
    tables = inner_tables(rows, total)
    outer = np.array([reversed_bits(a, levels) for a in range(devices)])
    twiddle = np.exp(-2j * np.pi / total * (outer[:, None] * np.arange(rows)[None, :] % total))
    factors = [jnp.asarray(parts(own, far)) for _, own, far, _, _ in stages[:-1]]
    _, own, far, _, phase = stages[-1]
    own, far = (own * phase)[:, None] * twiddle, (far * phase)[:, None] * twiddle
    factors.append(jnp.asarray(parts(own, far)))
    half, near_own, near_far = stages[-2][:3]
    flip = np.arange(devices) ^ stages[-1][0]
    direct = [own * near_own[:, None], own * near_far[:, None]]
    direct += [far * near_own[flip, None], far * near_far[flip, None]]
    partners = [half, stages[-1][0], half ^ stages[-1][0]]
    factors.append(jnp.asarray(parts(*direct)))
    numbers = [2 if stages[s + 1][3] else 1 for s in range(levels - 1)]

    chunks = column_chunks(count)

    def send(value, half):
        return lax.ppermute(value, "row", [(a, a ^ half) for a in range(devices)])

    out, far, results = {}, {}, {}
    stage_of = {"stencil": 0, "first": 1, "middle": levels - 1, "inner": levels}

    def is_direct(chunk):
        return chunk >= len(chunks) - DIRECT

    def after(name, chunk):
        kept = []
        for what, shift in ORDER[name]:
            at = chunk + shift - (name == "gate" and chunk == len(chunks) - 1)
            if 0 <= at < len(chunks):
                if what == "arrived":
                    make(0, at)
                    kept.append(far[0, at][0])
                elif stage_of[what] != levels - 1 or not is_direct(at):
                    make(stage_of[what], at)
                    kept.append(out[stage_of[what], at])
        return kept

    def make(stage, chunk):
        if (stage, chunk) in out:
            return
        block, number = chunks[chunk]
        if stage == 0:
            left = (before, 0) if block == 0 else (signal, block - 1)
            right = (behind, 0) if block == count - 1 else (signal, block + 1)
            out[stage, chunk] = stencil(
                left,
                (signal, block),
                right,
                apod[None, :],
                coef,
                fine_start[None, :],
                block_offset,
                block,
                number,
                after("stencil", chunk),
                VMEM if chunk else FIRST_VMEM,
            )
            waits = after("gate", chunk)
            if waits:
                out[stage, chunk] = gate(out[stage, chunk], waits)
        else:
            source = levels - 2 if stage == levels and is_direct(chunk) else stage - 1
            make(source, chunk)
            near, there = out[source, chunk], far[source, chunk]
            if stage < levels:
                out[stage, chunk] = combine(
                    me,
                    factors[stage - 1],
                    near,
                    there[0],
                    numbers[stage - 1],
                    after("first" if stage == 1 else "middle", chunk),
                )
            else:
                if chunk:
                    make(stage, chunk - 1)
                results[chunk], out[stage, chunk] = inner(
                    me,
                    factors[len(there) // 2 + levels - 1],
                    tables,
                    [near, *there],
                    results.get(chunk - 1),
                    block,
                    width,
                    after("inner", chunk),
                )
        if stage < levels:
            ways = partners if stage == levels - 2 and is_direct(chunk) else [stages[stage][0]]
            far[stage, chunk] = [send(out[stage, chunk], half) for half in ways]

    make(levels, len(chunks) - 1)
    return results[len(chunks) - 1]


def solution(mesh):
    placed = (P("row", "col"), P("row"), P(None, "col"), P("col"), P("col"))
    return jax.shard_map(
        on_device, mesh=mesh, in_specs=placed, out_specs=P(None, "row", "col"), check_vma=False
    )
```

```python
import functools
import math

import jax
import jax.numpy as jnp
import numpy as np
from jax import lax
from jax.experimental import pallas as pl
from jax.experimental.pallas import tpu as pltpu
from jax.sharding import PartitionSpec as P

TAPS = 4
LANES = 128
DIRECT = 2
SIZES = (1, 1, 1, 1, 1, 1)
ORDER = {
    "stencil": [],
    "gate": [("arrived", -1)],
    "first": [],
    "middle": [("stencil", 2), ("inner", -2)],
    "inner": [],
}
MIB = 1024 * 1024
VMEM = 20 * MIB
GATE_VMEM = 1 * MIB
FIRST_VMEM = 56 * MIB
QUICK = pl.CostEstimate(flops=0, bytes_accessed=0, transcendentals=0)


def split_bf16(value):
    high = value.astype(jnp.bfloat16)
    low = (value - high.astype(jnp.float32)).astype(jnp.bfloat16)
    return high, low


def dot3(a, b):
    dot = functools.partial(jnp.dot, preferred_element_type=jnp.float32)
    return dot(a[0], b[0]) + (dot(a[0], b[1]) + dot(a[1], b[0]))


def stencil_kernel(first, per_block, offsets, left, mid, right, apod, coef, fine, *rest):
    out = rest[-1]
    rows = mid.shape[0]
    block = first + pl.program_id(0)
    lane = lax.broadcasted_iota(jnp.int32, (1, LANES), 1)
    start = fine[...]
    if per_block >= LANES:
        start = start + offsets[block * LANES // per_block]
    else:
        for part in range(LANES // per_block):
            value = offsets[block * (LANES // per_block) + part]
            start = start + jnp.where(lane // per_block == part, value, 0)
    shape = (3 * LANES, LANES)
    tap_at = (
        lax.broadcasted_iota(jnp.int32, shape, 0)
        - lax.broadcasted_iota(jnp.int32, shape, 1)
        - LANES
        - start
    )
    band = jnp.zeros(shape, jnp.float32)
    for tap in range(TAPS):
        band = jnp.where(tap_at == tap, coef[tap : tap + 1, :], band)
    field = jnp.concatenate([left[...], mid[...], right[...]], axis=1)
    window = jnp.broadcast_to(apod[...], (LANES, rows)).T
    out[0] = window * dot3(split_bf16(field), split_bf16(band))


def stencil(left, mid, right, apod, coef, fine, offsets, block, count, after, vmem=VMEM):
    rows, width = mid[0].shape

    def columns(height, at):
        return pl.BlockSpec((height, LANES), lambda i: (0, at + i))

    return pl.pallas_call(
        functools.partial(stencil_kernel, block, width // offsets.shape[0]),
        grid=(count,),
        in_specs=[pl.BlockSpec(memory_space=pltpu.SMEM)]
        + [columns(rows, at) for _, at in (left, mid, right)]
        + [
            pl.BlockSpec((1, rows), lambda i: (0, 0)),
            columns(TAPS, block),
            columns(1, block),
        ]
        + [pl.BlockSpec(memory_space=pl.ANY)] * len(after),
        out_specs=pl.BlockSpec((1, rows, LANES), lambda i: (0, 0, i)),
        out_shape=jax.ShapeDtypeStruct((1, rows, count * LANES), jnp.float32),
        compiler_params=pltpu.CompilerParams(vmem_limit_bytes=vmem),
        cost_estimate=QUICK,
        name="stencil",
    )(offsets, left[0], mid[0], right[0], apod, coef, fine, *after)


def gate_kernel(value, *rest):
    pass


def gate(value, after):
    anywhere = pl.BlockSpec(memory_space=pl.ANY)
    return pl.pallas_call(
        gate_kernel,
        in_specs=[anywhere] * (1 + len(after)),
        out_specs=anywhere,
        out_shape=jax.ShapeDtypeStruct(value.shape, value.dtype),
        input_output_aliases={0: 0},
        compiler_params=pltpu.CompilerParams(vmem_limit_bytes=GATE_VMEM),
        cost_estimate=QUICK,
        name="gate",
    )(value, *after)


def combine_kernel(me, factors, own, far, *rest):
    out = rest[-1]
    a_re, a_im, b_re, b_im = (factors[me[0], i] for i in range(4))
    if own.shape[0] == 2:
        out[0] = a_re * own[0] - a_im * own[1] + (b_re * far[0] - b_im * far[1])
        out[1] = a_re * own[1] + a_im * own[0] + (b_re * far[1] + b_im * far[0])
    elif out.shape[0] == 2:
        out[0] = a_re * own[0] + b_re * far[0]
        out[1] = a_im * own[0] + b_im * far[0]
    else:
        out[0] = a_re * own[0] + b_re * far[0]


def combine(me, factors, own, far, number, after):
    whole = pl.BlockSpec(memory_space=pltpu.VMEM)
    small = pl.BlockSpec(memory_space=pltpu.SMEM)
    return pl.pallas_call(
        combine_kernel,
        in_specs=[small, small, whole, whole] + [pl.BlockSpec(memory_space=pl.ANY)] * len(after),
        out_specs=whole,
        out_shape=jax.ShapeDtypeStruct((number,) + own.shape[1:], jnp.float32),
        compiler_params=pltpu.CompilerParams(vmem_limit_bytes=VMEM),
        cost_estimate=QUICK,
        name="combine",
    )(me, factors, own, far, *after)


def inner_kernel(count, me, factors, cos_high, cos_low, sin_high, sin_low, *rest):
    out, token = rest[-2:]
    y_re = y_im = 0.0
    for i, block in enumerate(rest[:count]):
        f_re, f_im = (factors[0, :, 2 * i + j : 2 * i + j + 1] for j in range(2))
        y_re += f_re * block[0]
        y_im += f_im * block[0]
        if block.shape[0] == 2:
            y_re -= f_im * block[1]
            y_im += f_re * block[1]
    both = split_bf16(jnp.concatenate([y_re, y_im], axis=1))
    cos_part = dot3((cos_high[...], cos_low[...]), both)
    sin_part = dot3((sin_high[...], sin_low[...]), both)
    out[0] = cos_part[:, :LANES] + sin_part[:, LANES:]
    out[1] = cos_part[:, LANES:] - sin_part[:, :LANES]
    token[...] = jnp.zeros_like(token)


def inner(me, factors, tables, blocks, result, block, full_width, after):
    number, rows, width = blocks[0].shape
    kept = [] if result is None else [result]
    inputs = [me, factors, *tables, *blocks, *after, *kept]
    specs = (
        [pl.BlockSpec((1,) + factors.shape[1:], lambda i, at: (at[0], 0, 0))]
        + [pl.BlockSpec((rows, rows), lambda i, at: (0, 0))] * 4
        + [pl.BlockSpec((number, rows, LANES), lambda i, at: (0, 0, i))] * len(blocks)
        + [pl.BlockSpec(memory_space=pl.ANY)] * (len(after) + len(kept))
    )
    return pl.pallas_call(
        functools.partial(inner_kernel, len(blocks)),
        grid_spec=pltpu.PrefetchScalarGridSpec(
            num_scalar_prefetch=1,
            grid=(width // LANES,),
            in_specs=specs,
            out_specs=[
                pl.BlockSpec((2, rows, LANES), lambda i, at: (0, 0, block + i)),
                pl.BlockSpec((8, LANES), lambda i, at: (0, 0)),
            ],
        ),
        out_shape=[
            jax.ShapeDtypeStruct((2, rows, full_width), jnp.float32),
            jax.ShapeDtypeStruct((8, LANES), jnp.float32),
        ],
        input_output_aliases={len(inputs) - 1: 0} if kept else {},
        compiler_params=pltpu.CompilerParams(vmem_limit_bytes=VMEM),
        cost_estimate=QUICK,
        name="inner",
    )(*inputs)


def column_chunks(count):
    chunks, at = [], 1
    while at < count - 1:
        size = SIZES[min(len(chunks), len(SIZES) - 1)]
        chunks.append((at, min(size, count - 1 - at)))
        at += size
    return chunks + [(0, 1), (count - 1, 1)]


def reversed_bits(value, levels):
    return sum((value >> i & 1) << levels - 1 - i for i in range(levels))


def butterfly_plan(devices):
    stages = []
    phase = np.ones(devices, np.complex128)
    is_real = [True] * devices
    half = devices // 2
    while half:
        own, far = np.zeros(devices, np.complex128), np.zeros(devices, np.complex128)
        next_phase, next_real = phase.copy(), list(is_real)
        for a in range(devices):
            b = a ^ half
            upper = bool(a & half)
            turn = np.exp(-2j * np.pi * (a % half) / (2 * half)) if upper else 1.0
            keep = is_real[a] and phase[a] == 1 and phase[b] == 1
            if keep:
                own[a], far[a] = (-1 if upper else 1), 1
                next_phase[a] = turn
            else:
                own[a] = phase[a] * (-turn if upper else 1)
                far[a] = phase[b] * turn
                next_phase[a], next_real[a] = 1, False
        stages.append((half, own, far, [a for a in range(devices) if not is_real[a]], next_phase))
        phase, is_real = next_phase, next_real
        half //= 2
    return stages


def inner_tables(count, total):
    index = np.arange(count)
    angle = 2 * np.pi / count * (index[:, None] * index[None, :] % count)
    tables = []
    for part in (np.cos(angle), np.sin(angle)):
        part = part / math.sqrt(total)
        high = part.astype(jnp.bfloat16)
        tables += [high, (part - high.astype(np.float64)).astype(jnp.bfloat16)]
    return [jnp.asarray(t) for t in tables]


def parts(*values):
    return np.stack([p for v in values for p in (v.real, v.imag)], -1).astype(np.float32)


def on_device(signal, apod, coef, block_offset, fine_start):
    rows, width = signal.shape
    devices = lax.axis_size("row")
    me = lax.axis_index("row").astype(jnp.int32)[None]
    levels = devices.bit_length() - 1
    total = rows * devices
    count = width // LANES

    neighbours = lax.axis_size("col")
    up = [(i, i + 1) for i in range(neighbours - 1)]
    down = [(j, i) for i, j in up]
    before = lax.ppermute(signal[:, width - LANES :], "col", up)
    behind = lax.ppermute(signal[:, :LANES], "col", down)

    stages = butterfly_plan(devices)
    tables = inner_tables(rows, total)
    outer = np.array([reversed_bits(a, levels) for a in range(devices)])
    twiddle = np.exp(-2j * np.pi / total * (outer[:, None] * np.arange(rows)[None, :] % total))
    factors = [jnp.asarray(parts(own, far)) for _, own, far, _, _ in stages[:-1]]
    _, own, far, _, phase = stages[-1]
    own, far = (own * phase)[:, None] * twiddle, (far * phase)[:, None] * twiddle
    factors.append(jnp.asarray(parts(own, far)))
    half, near_own, near_far = stages[-2][:3]
    flip = np.arange(devices) ^ stages[-1][0]
    direct = [own * near_own[:, None], own * near_far[:, None]]
    direct += [far * near_own[flip, None], far * near_far[flip, None]]
    partners = [half, stages[-1][0], half ^ stages[-1][0]]
    factors.append(jnp.asarray(parts(*direct)))
    numbers = [2 if stages[s + 1][3] else 1 for s in range(levels - 1)]

    chunks = column_chunks(count)

    def send(value, half):
        return lax.ppermute(value, "row", [(a, a ^ half) for a in range(devices)])

    out, far, results = {}, {}, {}
    stage_of = {"stencil": 0, "first": 1, "middle": levels - 1, "inner": levels}

    def is_direct(chunk):
        return chunk >= len(chunks) - DIRECT

    def after(name, chunk):
        kept = []
        for what, shift in ORDER[name]:
            at = chunk + shift
            if 0 <= at < len(chunks):
                if what == "arrived":
                    make(0, at)
                    kept.append(far[0, at][0])
                elif stage_of[what] != levels - 1 or not is_direct(at):
                    make(stage_of[what], at)
                    kept.append(out[stage_of[what], at])
        return kept

    def make(stage, chunk):
        if (stage, chunk) in out:
            return
        block, number = chunks[chunk]
        if stage == 0:
            left = (before, 0) if block == 0 else (signal, block - 1)
            right = (behind, 0) if block == count - 1 else (signal, block + 1)
            out[stage, chunk] = stencil(
                left,
                (signal, block),
                right,
                apod[None, :],
                coef,
                fine_start[None, :],
                block_offset,
                block,
                number,
                after("stencil", chunk),
                VMEM if chunk else FIRST_VMEM,
            )
            waits = after("gate", chunk)
            if waits:
                out[stage, chunk] = gate(out[stage, chunk], waits)
        else:
            source = levels - 2 if stage == levels and is_direct(chunk) else stage - 1
            make(source, chunk)
            near, there = out[source, chunk], far[source, chunk]
            if stage < levels:
                out[stage, chunk] = combine(
                    me,
                    factors[stage - 1],
                    near,
                    there[0],
                    numbers[stage - 1],
                    after("first" if stage == 1 else "middle", chunk),
                )
            else:
                if chunk:
                    make(stage, chunk - 1)
                results[chunk], out[stage, chunk] = inner(
                    me,
                    factors[len(there) // 2 + levels - 1],
                    tables,
                    [near, *there],
                    results.get(chunk - 1),
                    block,
                    width,
                    after("inner", chunk),
                )
        if stage < levels:
            ways = partners if stage == levels - 2 and is_direct(chunk) else [stages[stage][0]]
            far[stage, chunk] = [send(out[stage, chunk], half) for half in ways]

    make(levels, len(chunks) - 1)
    return results[len(chunks) - 1]


def solution(mesh):
    placed = (P("row", "col"), P("row"), P(None, "col"), P("col"), P("col"))
    return jax.shard_map(
        on_device, mesh=mesh, in_specs=placed, out_specs=P(None, "row", "col"), check_vma=False
    )
```

```python
import functools
import math

import jax
import jax.numpy as jnp
import numpy as np
from jax import lax
from jax.experimental import pallas as pl
from jax.experimental.pallas import tpu as pltpu
from jax.sharding import PartitionSpec as P

TAPS = 4
LANES = 128
DIRECT = 2
SIZES = (1, 1, 1, 1, 1, 1)
ORDER = {'stencil': [], 'gate': [('arrived', -1)], 'first': [('middle', -1)], 'middle': [('stencil', 2), ('inner', -2)], 'inner': [('middle', 1), ('first', 2)]}
MIB = 1024 * 1024
VMEM = 20 * MIB
GATE_VMEM = 1 * MIB
FIRST_VMEM = 56 * MIB
QUICK = pl.CostEstimate(flops=0, bytes_accessed=0, transcendentals=0)


def split_bf16(value):
    high = value.astype(jnp.bfloat16)
    low = (value - high.astype(jnp.float32)).astype(jnp.bfloat16)
    return high, low


def dot3(a, b):
    dot = functools.partial(jnp.dot, preferred_element_type=jnp.float32)
    return dot(a[0], b[0]) + (dot(a[0], b[1]) + dot(a[1], b[0]))


def stencil_kernel(first, per_block, offsets, left, mid, right, apod, coef, fine, *rest):
    out = rest[-1]
    rows = mid.shape[0]
    block = first + pl.program_id(0)
    lane = lax.broadcasted_iota(jnp.int32, (1, LANES), 1)
    start = fine[...]
    if per_block >= LANES:
        start = start + offsets[block * LANES // per_block]
    else:
        for part in range(LANES // per_block):
            value = offsets[block * (LANES // per_block) + part]
            start = start + jnp.where(lane // per_block == part, value, 0)
    shape = (3 * LANES, LANES)
    tap_at = (
        lax.broadcasted_iota(jnp.int32, shape, 0)
        - lax.broadcasted_iota(jnp.int32, shape, 1)
        - LANES
        - start
    )
    band = jnp.zeros(shape, jnp.float32)
    for tap in range(TAPS):
        band = jnp.where(tap_at == tap, coef[tap : tap + 1, :], band)
    field = jnp.concatenate([left[...], mid[...], right[...]], axis=1)
    window = jnp.broadcast_to(apod[...], (LANES, rows)).T
    out[0] = window * dot3(split_bf16(field), split_bf16(band))


def stencil(left, mid, right, apod, coef, fine, offsets, block, count, after, vmem=VMEM):
    rows, width = mid[0].shape

    def columns(height, at):
        return pl.BlockSpec((height, LANES), lambda i: (0, at + i))

    return pl.pallas_call(
        functools.partial(stencil_kernel, block, width // offsets.shape[0]),
        grid=(count,),
        in_specs=[pl.BlockSpec(memory_space=pltpu.SMEM)]
        + [columns(rows, at) for _, at in (left, mid, right)]
        + [
            pl.BlockSpec((1, rows), lambda i: (0, 0)),
            columns(TAPS, block),
            columns(1, block),
        ]
        + [pl.BlockSpec(memory_space=pl.ANY)] * len(after),
        out_specs=pl.BlockSpec((1, rows, LANES), lambda i: (0, 0, i)),
        out_shape=jax.ShapeDtypeStruct((1, rows, count * LANES), jnp.float32),
        compiler_params=pltpu.CompilerParams(vmem_limit_bytes=vmem),
        cost_estimate=QUICK,
        name="stencil",
    )(offsets, left[0], mid[0], right[0], apod, coef, fine, *after)


def gate_kernel(value, *rest):
    pass


def gate(value, after):
    anywhere = pl.BlockSpec(memory_space=pl.ANY)
    return pl.pallas_call(
        gate_kernel,
        in_specs=[anywhere] * (1 + len(after)),
        out_specs=anywhere,
        out_shape=jax.ShapeDtypeStruct(value.shape, value.dtype),
        input_output_aliases={0: 0},
        compiler_params=pltpu.CompilerParams(vmem_limit_bytes=GATE_VMEM),
        cost_estimate=QUICK,
        name="gate",
    )(value, *after)


def combine_kernel(me, factors, own, far, *rest):
    out = rest[-1]
    a_re, a_im, b_re, b_im = (factors[me[0], i] for i in range(4))
    if own.shape[0] == 2:
        out[0] = a_re * own[0] - a_im * own[1] + (b_re * far[0] - b_im * far[1])
        out[1] = a_re * own[1] + a_im * own[0] + (b_re * far[1] + b_im * far[0])
    elif out.shape[0] == 2:
        out[0] = a_re * own[0] + b_re * far[0]
        out[1] = a_im * own[0] + b_im * far[0]
    else:
        out[0] = a_re * own[0] + b_re * far[0]


def combine(me, factors, own, far, number, after):
    whole = pl.BlockSpec(memory_space=pltpu.VMEM)
    small = pl.BlockSpec(memory_space=pltpu.SMEM)
    return pl.pallas_call(
        combine_kernel,
        in_specs=[small, small, whole, whole] + [pl.BlockSpec(memory_space=pl.ANY)] * len(after),
        out_specs=whole,
        out_shape=jax.ShapeDtypeStruct((number,) + own.shape[1:], jnp.float32),
        compiler_params=pltpu.CompilerParams(vmem_limit_bytes=VMEM),
        cost_estimate=QUICK,
        name="combine",
    )(me, factors, own, far, *after)


def inner_kernel(count, me, factors, cos_high, cos_low, sin_high, sin_low, *rest):
    out, token = rest[-2:]
    y_re = y_im = 0.0
    for i, block in enumerate(rest[:count]):
        f_re, f_im = (factors[0, :, 2 * i + j : 2 * i + j + 1] for j in range(2))
        y_re += f_re * block[0]
        y_im += f_im * block[0]
        if block.shape[0] == 2:
            y_re -= f_im * block[1]
            y_im += f_re * block[1]
    both = split_bf16(jnp.concatenate([y_re, y_im], axis=1))
    cos_part = dot3((cos_high[...], cos_low[...]), both)
    sin_part = dot3((sin_high[...], sin_low[...]), both)
    out[0] = cos_part[:, :LANES] + sin_part[:, LANES:]
    out[1] = cos_part[:, LANES:] - sin_part[:, :LANES]
    token[...] = jnp.zeros_like(token)


def inner(me, factors, tables, blocks, result, block, full_width, after):
    number, rows, width = blocks[0].shape
    kept = [] if result is None else [result]
    inputs = [me, factors, *tables, *blocks, *after, *kept]
    specs = (
        [pl.BlockSpec((1,) + factors.shape[1:], lambda i, at: (at[0], 0, 0))]
        + [pl.BlockSpec((rows, rows), lambda i, at: (0, 0))] * 4
        + [pl.BlockSpec((number, rows, LANES), lambda i, at: (0, 0, i))] * len(blocks)
        + [pl.BlockSpec(memory_space=pl.ANY)] * (len(after) + len(kept))
    )
    return pl.pallas_call(
        functools.partial(inner_kernel, len(blocks)),
        grid_spec=pltpu.PrefetchScalarGridSpec(
            num_scalar_prefetch=1,
            grid=(width // LANES,),
            in_specs=specs,
            out_specs=[
                pl.BlockSpec((2, rows, LANES), lambda i, at: (0, 0, block + i)),
                pl.BlockSpec((8, LANES), lambda i, at: (0, 0)),
            ],
        ),
        out_shape=[
            jax.ShapeDtypeStruct((2, rows, full_width), jnp.float32),
            jax.ShapeDtypeStruct((8, LANES), jnp.float32),
        ],
        input_output_aliases={len(inputs) - 1: 0} if kept else {},
        compiler_params=pltpu.CompilerParams(vmem_limit_bytes=VMEM),
        cost_estimate=QUICK,
        name="inner",
    )(*inputs)


def column_chunks(count):
    chunks, at = [], 1
    while at < count - 1:
        size = SIZES[min(len(chunks), len(SIZES) - 1)]
        chunks.append((at, min(size, count - 1 - at)))
        at += size
    return chunks + [(0, 1), (count - 1, 1)]


def reversed_bits(value, levels):
    return sum((value >> i & 1) << levels - 1 - i for i in range(levels))


def butterfly_plan(devices):
    stages = []
    phase = np.ones(devices, np.complex128)
    is_real = [True] * devices
    half = devices // 2
    while half:
        own, far = np.zeros(devices, np.complex128), np.zeros(devices, np.complex128)
        next_phase, next_real = phase.copy(), list(is_real)
        for a in range(devices):
            b = a ^ half
            upper = bool(a & half)
            turn = np.exp(-2j * np.pi * (a % half) / (2 * half)) if upper else 1.0
            keep = is_real[a] and phase[a] == 1 and phase[b] == 1
            if keep:
                own[a], far[a] = (-1 if upper else 1), 1
                next_phase[a] = turn
            else:
                own[a] = phase[a] * (-turn if upper else 1)
                far[a] = phase[b] * turn
                next_phase[a], next_real[a] = 1, False
        stages.append((half, own, far, [a for a in range(devices) if not is_real[a]], next_phase))
        phase, is_real = next_phase, next_real
        half //= 2
    return stages


def inner_tables(count, total):
    index = np.arange(count)
    angle = 2 * np.pi / count * (index[:, None] * index[None, :] % count)
    tables = []
    for part in (np.cos(angle), np.sin(angle)):
        part = part / math.sqrt(total)
        high = part.astype(jnp.bfloat16)
        tables += [high, (part - high.astype(np.float64)).astype(jnp.bfloat16)]
    return [jnp.asarray(t) for t in tables]


def parts(*values):
    return np.stack([p for v in values for p in (v.real, v.imag)], -1).astype(np.float32)


def on_device(signal, apod, coef, block_offset, fine_start):
    rows, width = signal.shape
    devices = lax.axis_size("row")
    me = lax.axis_index("row").astype(jnp.int32)[None]
    levels = devices.bit_length() - 1
    total = rows * devices
    count = width // LANES

    neighbours = lax.axis_size("col")
    up = [(i, i + 1) for i in range(neighbours - 1)]
    down = [(j, i) for i, j in up]
    before = lax.ppermute(signal[:, width - LANES :], "col", up)
    behind = lax.ppermute(signal[:, :LANES], "col", down)

    stages = butterfly_plan(devices)
    tables = inner_tables(rows, total)
    outer = np.array([reversed_bits(a, levels) for a in range(devices)])
    twiddle = np.exp(-2j * np.pi / total * (outer[:, None] * np.arange(rows)[None, :] % total))
    factors = [jnp.asarray(parts(own, far)) for _, own, far, _, _ in stages[:-1]]
    _, own, far, _, phase = stages[-1]
    own, far = (own * phase)[:, None] * twiddle, (far * phase)[:, None] * twiddle
    factors.append(jnp.asarray(parts(own, far)))
    half, near_own, near_far = stages[-2][:3]
    flip = np.arange(devices) ^ stages[-1][0]
    direct = [own * near_own[:, None], own * near_far[:, None]]
    direct += [far * near_own[flip, None], far * near_far[flip, None]]
    partners = [half, stages[-1][0], half ^ stages[-1][0]]
    factors.append(jnp.asarray(parts(*direct)))
    numbers = [2 if stages[s + 1][3] else 1 for s in range(levels - 1)]

    chunks = column_chunks(count)

    def send(value, half):
        return lax.ppermute(value, "row", [(a, a ^ half) for a in range(devices)])

    out, far, results = {}, {}, {}
    stage_of = {"stencil": 0, "first": 1, "middle": levels - 1, "inner": levels}

    def is_direct(chunk):
        return chunk >= len(chunks) - DIRECT

    def after(name, chunk):
        kept = []
        for what, shift in ORDER[name]:
            at = chunk + shift
            if 0 <= at < len(chunks):
                if what == "arrived":
                    make(0, at)
                    kept.append(far[0, at][0])
                elif stage_of[what] != levels - 1 or not is_direct(at):
                    make(stage_of[what], at)
                    kept.append(out[stage_of[what], at])
        return kept

    def make(stage, chunk):
        if (stage, chunk) in out:
            return
        block, number = chunks[chunk]
        if stage == 0:
            left = (before, 0) if block == 0 else (signal, block - 1)
            right = (behind, 0) if block == count - 1 else (signal, block + 1)
            out[stage, chunk] = stencil(
                left,
                (signal, block),
                right,
                apod[None, :],
                coef,
                fine_start[None, :],
                block_offset,
                block,
                number,
                after("stencil", chunk),
                VMEM if chunk else FIRST_VMEM,
            )
            waits = after("gate", chunk)
            if waits:
                out[stage, chunk] = gate(out[stage, chunk], waits)
        else:
            source = levels - 2 if stage == levels and is_direct(chunk) else stage - 1
            make(source, chunk)
            near, there = out[source, chunk], far[source, chunk]
            if stage < levels:
                out[stage, chunk] = combine(
                    me,
                    factors[stage - 1],
                    near,
                    there[0],
                    numbers[stage - 1],
                    after("first" if stage == 1 else "middle", chunk),
                )
            else:
                if chunk:
                    make(stage, chunk - 1)
                results[chunk], out[stage, chunk] = inner(
                    me,
                    factors[len(there) // 2 + levels - 1],
                    tables,
                    [near, *there],
                    results.get(chunk - 1),
                    block,
                    width,
                    after("inner", chunk),
                )
        if stage < levels:
            ways = partners if stage == levels - 2 and is_direct(chunk) else [stages[stage][0]]
            far[stage, chunk] = [send(out[stage, chunk], half) for half in ways]

    make(levels, len(chunks) - 1)
    return results[len(chunks) - 1]


def solution(mesh):
    placed = (P("row", "col"), P("row"), P(None, "col"), P("col"), P("col"))
    return jax.shard_map(
        on_device, mesh=mesh, in_specs=placed, out_specs=P(None, "row", "col"), check_vma=False
    )
```
